32 devices in a mesh: site: 4 (over y, x), term: 8 (over z, core).
Axes of the slice: x: 2, y: 2, z: 4, core: 2. Of those that a mesh axis runs over, the one named last changes fastest.
Arguments:
- left_env: float32 [8, 12, 256, 256], P('term'), may hold values from -6 to 6
- right_env: float32 [4, 8, 12, 256, 256], P('site', 'term'), may hold values from -6 to 6
- mps: float32 [4, 2, 12, 256, 256], P('site'), may hold values from -0.375 to 0.375
- psi: float32 [4, 2, 12, 256, 256], P('site'), may hold values from -0.0078125 to 0.0078125
- coef: float32 [4, 8, 4], P('site', 'term'), may hold values from 0.5 to 1.5
- sector_sizes: int32 [12], replicated, may hold values from 128 to 256, as said below
- pattern: int32 [8, 12], P('term'), may hold values 0 or 1
Outputs:
- applied: float32 [4, 2, 3072, 256], P('site', None, 'term')
The draws below stay inside these ranges and needn't reach their ends.
Inputs may be any that keep to these rules, and one draw needn't show every extreme that they name: `sector_sizes`: every size lies in 128 .. 256, the sizes add up to exactly 2560, and at least one sector has exactly 256.
All inputs are finite; a program needn't handle non-finite values. No bound on the sum of `pattern` on one device may be relied on, other than what follows from the above.
Results may differ from the reference program's by a relative error of at most 0.00018.
Values sent between devices are 32-bit elements; how exact they have to be, the bound alone decides.
A program may use at most 128 MiB of HBM per device.

```python
import jax
import jax.numpy as jnp
from jax import lax

NSEC = 12
P_SIZE = 256
BOND = 2560
TERMS = 8
N_SITE = 4


def draw_sector_sizes(key, part):
    first_key, second_key = jax.random.split(jax.random.fold_in(key, 17))
    lowest = P_SIZE // 2
    spare_rows = BOND - NSEC * lowest - lowest
    full_slot = jax.random.randint(first_key, (), 0, NSEC)
    unit_slots = jax.random.permutation(second_key, (NSEC - 1) * lowest)[:spare_rows] // lowest
    counts_other = jnp.sum((unit_slots[None, :] == jnp.arange(NSEC - 1)[:, None]).astype(jnp.int32), axis=1)
    others = lowest + counts_other
    slot_index = jnp.arange(NSEC)
    source = jnp.clip(slot_index - (slot_index > full_slot).astype(jnp.int32), 0, NSEC - 2)
    return jnp.where(slot_index == full_slot, P_SIZE, others[source]).astype(jnp.int32)


def plant(entries, own_key, low, top_value):
    dims = entries.shape
    place = [jax.random.randint(jax.random.fold_in(own_key, axis), (), 0, dims[axis]) for axis in range(len(dims))]
    entries = entries.at[tuple(place)].set(low)
    longest = dims.index(max(dims))
    place[longest] = (place[longest] + 1) % dims[longest]
    return entries.at[tuple(place)].set(top_value)


def level_of(stream_key, shape, cuts, low, top_value):
    gain = 1.0
    for position, blocks in cuts:
        heights = jax.random.uniform(jax.random.fold_in(jax.random.fold_in(stream_key, 6), position), (blocks,), jnp.float32, low / len(cuts), top_value / len(cuts))
        gain = gain * jnp.repeat(jnp.exp(heights), shape[position] // blocks).reshape((-1,) + (1,) * (len(shape) - 1 - position))
    return gain


def normal_values(own_key, dims, width, most, cuts=(), held_as=jnp.bfloat16):
    factor_of = level_of(own_key, dims, cuts, -0.22, 0.18) if cuts else 1.0
    drawn = jax.random.normal(own_key, dims, jnp.float32) * width * factor_of
    return jnp.minimum(jnp.maximum(drawn, -most), most).astype(held_as)


def setup_inputs(seed: int = 0) -> dict:
    splits = jax.random.split(jax.random.key(seed), 8)
    return {
        "left_env": normal_values(splits[0], (TERMS, NSEC, P_SIZE, P_SIZE), 1.0, 6.0, ((0, 8),), jnp.float32),
        "right_env": normal_values(splits[1], (N_SITE, TERMS, NSEC, P_SIZE, P_SIZE), 1.0, 6.0, ((0, 4), (1, 8)), jnp.float32),
        "mps": normal_values(splits[2], (N_SITE, 2, NSEC, P_SIZE, P_SIZE), P_SIZE ** -0.5, 0.375, ((0, 4),), jnp.float32),
        "psi": normal_values(splits[3], (N_SITE, 2, NSEC, P_SIZE, P_SIZE), (P_SIZE * P_SIZE * TERMS) ** -0.5, 0.0078125, ((0, 4),), jnp.float32),
        "coef": jnp.clip(0.5 + 1.0 * jax.random.uniform(splits[4], (N_SITE, TERMS, 4), jnp.float32) ** level_of(splits[4], (N_SITE, TERMS, 4), ((0, 4), (1, 8)), -0.2, 0.2), 0.5, 1.5),
        "sector_sizes": draw_sector_sizes(jax.random.fold_in(splits[7], 71), 0),
        "pattern": plant((jax.random.randint(splits[6], (TERMS, NSEC), 0, 4) < 3).astype(jnp.int32), jax.random.fold_in(splits[6], 1), 0, 1),
    }


highest = lax.Precision.HIGHEST


def live_masks(sector_sizes):
    live_rows = (jnp.arange(P_SIZE)[None, :] < sector_sizes[:, None]).astype(jnp.float32)
    following = jnp.concatenate([live_rows[1:], jnp.zeros((1, P_SIZE), jnp.float32)], axis=0)
    sector_frame = live_rows[:, :, None] * live_rows[:, None, :]
    step_frame = live_rows[:, :, None] * following[:, None, :]
    return sector_frame, step_frame


def sandwich(blocks, tensors):
    product = jnp.einsum("nij,njk->nik", blocks, tensors, precision=highest)
    return jnp.einsum("nim,nik->nmk", tensors, product, precision=highest)


def advance(environ, weights, same_state, next_state):
    shifted = jnp.concatenate([jnp.zeros((1, P_SIZE, P_SIZE), jnp.float32), environ[:-1]], axis=0)
    rolled = jnp.roll(next_state, 1, axis=0)
    return weights[0] * sandwich(environ, same_state) + weights[1] * sandwich(shifted, rolled)


def reference(left_env, right_env, mps, psi, coef, sector_sizes, pattern):
    sector_frame, step_frame = live_masks(sector_sizes)
    presence = pattern.astype(jnp.float32)[:, :, None, None]
    environ = left_env * sector_frame[None] * presence
    results = []
    for section_index in range(N_SITE):
        same_state = mps[section_index, 0] * sector_frame
        next_state = mps[section_index, 1] * step_frame

        def update_term(operands):
            return advance(operands[0], operands[1], same_state, next_state)

        environ = lax.map(update_term, (environ, coef[section_index]))
        rights = right_env[section_index] * sector_frame[None] * presence
        first_psi = psi[section_index, 0] * sector_frame
        second_psi = psi[section_index, 1] * step_frame

        def accumulate(totals, pieces):
            left_blocks, right_blocks, weights = pieces
            upper_blocks = jnp.concatenate([right_blocks[1:], jnp.zeros((1, P_SIZE, P_SIZE), jnp.float32)], axis=0)
            first_term = jnp.einsum("qij,qjk->qik", left_blocks, first_psi, precision=highest)
            first_term = jnp.einsum("qik,qlk->qil", first_term, right_blocks, precision=highest)
            second = jnp.einsum("qij,qjk->qik", left_blocks, second_psi, precision=highest)
            second = jnp.einsum("qik,qlk->qil", second, upper_blocks, precision=highest)
            return (totals[0] + weights[2] * first_term, totals[1] + weights[3] * second), None

        empty_sum = jnp.zeros((NSEC, P_SIZE, P_SIZE), jnp.float32)
        sums, ignored = lax.scan(accumulate, (empty_sum, empty_sum), (environ, rights, coef[section_index]))
        results.append(jnp.stack([sums[0].reshape(NSEC * P_SIZE, P_SIZE), sums[1].reshape(NSEC * P_SIZE, P_SIZE)]))
    return jnp.stack(results)
```

```python
import functools
import math

import jax
import jax.numpy as jnp
from jax import lax
from jax.experimental import pallas as pl
from jax.experimental.pallas import tpu as pltpu
from jax.sharding import PartitionSpec as P

MESH = pl.DeviceIdType.MESH
FIRST_LAG = 1
HOP_LAG = 2


def halves(x):
    high = x.astype(jnp.bfloat16)
    return high, (x - high.astype(jnp.float32)).astype(jnp.bfloat16)


def product(a, b, left_dim=1, right_dim=0):
    def dot(x, y):
        return lax.dot_general(
            x, y, (((left_dim,), (right_dim,)), ((), ())), preferred_element_type=jnp.float32
        )

    return dot(a[0], b[0]) + (dot(a[0], b[1]) + dot(a[1], b[0]))


def sandwich(block, tensor):
    parts = halves(tensor)
    return product(parts, halves(product(halves(block), parts)), 0, 0)


def kernel(
    sites, terms, unit,
    left, right, mps, psi, coef, sizes, pattern, out,
    e_in, e_out, right_v, mps_v, psi_v, partial, pair_in, up_in, down_in,
    left_sem, right_sem, mps_sem, psi_sem,
    e_send, e_recv, pair_send, pair_recv, z_send, up_recv, down_recv,
):
    nsec, width = e_in.shape[0], e_in.shape[1]
    chips = terms // 2
    rows_owned = nsec * width // terms
    per = rows_owned // unit
    in_sector = width // unit
    site, term = lax.axis_index("site"), lax.axis_index("term")
    chip, core = term // 2, term % 2
    partner = chip * 2 + 1 - core

    def left_copy(q):
        return pltpu.make_async_copy(left.at[0, q], e_in.at[q], left_sem.at[q])

    def right_copy(q):
        return pltpu.make_async_copy(right.at[0, 0, q], right_v.at[q], right_sem.at[q])

    def mps_copy(q):
        return pltpu.make_async_copy(mps.at[0, :, q], mps_v.at[:, q], mps_sem.at[q])

    def psi_copy(q):
        return pltpu.make_async_copy(psi.at[0, :, q], psi_v.at[:, q], psi_sem.at[q])

    @pl.loop(0, nsec)
    def _(q):
        @pl.when(site == 0)
        def _():
            left_copy(q).start()

        mps_copy(q).start()
        psi_copy(q).start()
        right_copy(q).start()

    def e_copy(q):
        return pltpu.make_async_remote_copy(
            src_ref=e_out.at[q], dst_ref=e_in.at[q],
            send_sem=e_send.at[q], recv_sem=e_recv.at[q],
            device_id={"site": jnp.minimum(site + 1, sites - 1)}, device_id_type=MESH,
        )

    def pair_copy(piece, place):
        return pltpu.make_async_remote_copy(
            src_ref=partial.at[piece], dst_ref=pair_in.at[place],
            send_sem=pair_send.at[place], recv_sem=pair_recv.at[place],
            device_id={"term": partner}, device_id_type=MESH,
        )

    def up_copy(piece, place):
        return pltpu.make_async_remote_copy(
            src_ref=partial.at[piece], dst_ref=up_in.at[place],
            send_sem=z_send.at[place], recv_sem=up_recv.at[place],
            device_id={"term": jnp.minimum(term + 2, terms - 2 + core)}, device_id_type=MESH,
        )

    def down_copy(piece, place):
        return pltpu.make_async_remote_copy(
            src_ref=partial.at[piece], dst_ref=down_in.at[place],
            send_sem=z_send.at[place], recv_sem=down_recv.at[place],
            device_id={"term": jnp.maximum(term - 2, core)}, device_id_type=MESH,
        )

    barrier = pltpu.get_barrier_semaphore()
    greet = functools.partial(pl.semaphore_signal, barrier, inc=1, device_id_type=MESH)
    greet(device_id={"term": partner})
    pl.when(site > 0)(lambda: greet(device_id={"site": site - 1}))
    pl.when(site < sites - 1)(lambda: greet(device_id={"site": site + 1}))
    pl.when(chip > 0)(lambda: greet(device_id={"term": term - 2}))
    pl.when(chip < chips - 1)(lambda: greet(device_id={"term": term + 2}))
    bounds = (site > 0, site < sites - 1, chip > 0, chip < chips - 1)
    peers = 1
    for met in bounds:
        peers = peers + jnp.where(met, 1, 0)
    pl.semaphore_wait(barrier, peers)

    rows = lax.broadcasted_iota(jnp.int32, (width, width), 0)
    columns = lax.broadcasted_iota(jnp.int32, (width, width), 1)

    def framed(x, high, wide):
        return jnp.where((rows < high) & (columns < wide), x, 0.0)

    def where_of(piece):
        owner = piece // per
        place = (owner // 2) * per + piece % per
        return owner // 2, owner % 2, place

    right_copy(0).wait()

    def sector(q):
        before, after = jnp.maximum(q - 1, 0), jnp.minimum(q + 1, nsec - 1)
        mps_copy(q).wait()
        pl.when(site == 0)(lambda: left_copy(q).wait())
        pl.when(site > 0)(lambda: e_copy(q).wait_recv())

        size, size_before = sizes[q], sizes[before]
        size_after = jnp.where(q + 1 < nsec, sizes[after], 0)
        there = pattern[0, q].astype(jnp.float32)
        there_after = pattern[0, after].astype(jnp.float32)
        first = jnp.where(site == 0, there, 1.0)
        first_before = jnp.where(site == 0, pattern[0, before].astype(jnp.float32), 1.0)
        same = framed(mps_v[0, q], size, size)
        step = framed(mps_v[1, before], size_before, size)
        here = framed(e_in[q], size, size) * first
        shifted = framed(e_in[before], size_before, size_before) * first_before
        weight = jnp.where(q > 0, coef[0, 0, 1], 0.0)
        e_out[q] = coef[0, 0, 0] * sandwich(here, same) + weight * sandwich(shifted, step)
        pl.when(site < sites - 1)(lambda: e_copy(q).start())

        psi_copy(q).wait()
        pl.when(q + 1 < nsec)(lambda: right_copy(after).wait())
        environ = halves(e_out[q])
        for state, (held, size_r, there_r) in enumerate(
            ((q, size, there), (after, size_after, there_after))
        ):
            psi_block = framed(psi_v[state, q], size, size_r)
            block = framed(right_v[held], size_r, size_r) * there_r
            value = product(environ, halves(psi_block)) * coef[0, 0, 2 + state]
            value = product(halves(value), halves(block), 1, 1)
            for i in range(in_sector):
                partial[q * in_sector + i, state] = value[i * unit:(i + 1) * unit]

        for i in range(in_sector):
            piece = q * in_sector + i
            _, owner_core, place = where_of(piece)
            pl.when(owner_core != core)(lambda: pair_copy(piece, place).start())

    def upward(q):
        for i in range(in_sector):
            piece = q * in_sector + i
            owner_chip, owner_core, place = where_of(piece)

            @pl.when((owner_core == core) & (owner_chip > chip))
            def _():
                pair_copy(piece, place).wait_recv()

                @pl.when(chip == 0)
                def _():
                    partial[piece] = partial[piece] + pair_in[place]

                @pl.when(chip > 0)
                def _():
                    up_copy(piece, place).wait_recv()
                    partial[piece] = (partial[piece] + pair_in[place]) + up_in[place]

                up_copy(piece, place).start()

    def downward(q):
        for i in range(in_sector):
            piece = q * in_sector + i
            owner_chip, owner_core, place = where_of(piece)

            @pl.when((owner_core == core) & (owner_chip < chip))
            def _():
                pair_copy(piece, place).wait_recv()

                @pl.when(chip == chips - 1)
                def _():
                    partial[piece] = partial[piece] + pair_in[place]

                @pl.when(chip < chips - 1)
                def _():
                    down_copy(piece, place).wait_recv()
                    partial[piece] = (partial[piece] + pair_in[place]) + down_in[place]

                down_copy(piece, place).start()

    def ending(q):
        for i in range(in_sector):
            piece = q * in_sector + i
            owner_chip, owner_core, place = where_of(piece)

            @pl.when((owner_core == core) & (owner_chip == chip))
            def _():
                target = pl.ds(pl.multiple_of((piece % per) * unit, unit), unit)
                pair_copy(piece, place).wait_recv()
                out[0, :, target, :] = partial[piece] + pair_in[place]

                @pl.when(chip > 0)
                def _():
                    up_copy(piece, place).wait_recv()
                    out[0, :, target, :] = out[0, :, target, :] + up_in[place]

                @pl.when(chip < chips - 1)
                def _():
                    down_copy(piece, place).wait_recv()
                    out[0, :, target, :] = out[0, :, target, :] + down_in[place]

    from_below, from_above = chip, chips - 1 - chip

    def turn(t, carry):
        pl.when(t < nsec)(lambda: sector(t))
        for stage, hops in (
            (upward, from_below),
            (downward, from_above),
            (ending, jnp.maximum(from_below, from_above)),
        ):
            q = t - FIRST_LAG - hops * HOP_LAG
            pl.when((q >= 0) & (q < nsec))(lambda: stage(q))
        return carry

    lax.fori_loop(0, nsec + FIRST_LAG + (chips - 1) * HOP_LAG, turn, 0)

    @pl.loop(0, nsec)
    def _(q):
        pl.when(site < sites - 1)(lambda: e_copy(q).wait_send())
        for i in range(in_sector):
            piece = q * in_sector + i
            owner_chip, owner_core, place = where_of(piece)
            pl.when(owner_core != core)(lambda: pair_copy(piece, place).wait_send())
            mine = owner_core == core
            pl.when(mine & (owner_chip > chip))(lambda: up_copy(piece, place).wait_send())
            pl.when(mine & (owner_chip < chip))(lambda: down_copy(piece, place).wait_send())


def shards(left_env, right_env, mps, psi, coef, sector_sizes, pattern):
    nsec, width = left_env.shape[1], left_env.shape[-1]
    sites, terms = lax.axis_size("site"), lax.axis_size("term")
    rows_owned = nsec * width // terms
    unit = math.gcd(rows_owned, width)
    pieces = nsec * width // unit
    mine = pieces // 2
    block = (nsec, width, width)
    dma = pltpu.SemaphoreType.DMA
    hbm, smem = pl.BlockSpec(memory_space=pl.ANY), pl.BlockSpec(memory_space=pltpu.SMEM)
    return pl.pallas_call(
        functools.partial(kernel, sites, terms, unit),
        out_shape=jax.ShapeDtypeStruct((1, 2, rows_owned, width), jnp.float32),
        in_specs=[hbm] * 4 + [smem] * 3,
        out_specs=pl.BlockSpec(memory_space=pltpu.VMEM),
        scratch_shapes=[
            pltpu.VMEM(block, jnp.float32),
            pltpu.VMEM(block, jnp.float32),
            pltpu.VMEM(block, jnp.float32),
            pltpu.VMEM((2,) + block, jnp.float32),
            pltpu.VMEM((2,) + block, jnp.float32),
            pltpu.VMEM((pieces, 2, unit, width), jnp.float32),
            pltpu.VMEM((mine, 2, unit, width), jnp.float32),
            pltpu.VMEM((mine, 2, unit, width), jnp.float32),
            pltpu.VMEM((mine, 2, unit, width), jnp.float32),
            dma((nsec,)), dma((nsec,)), dma((nsec,)), dma((nsec,)),
            dma((nsec,)), dma((nsec,)),
            dma((mine,)), dma((mine,)), dma((mine,)), dma((mine,)), dma((mine,)),
        ],
        compiler_params=pltpu.CompilerParams(
            collective_id=0, has_side_effects=True, vmem_limit_bytes=56 * 2**20
        ),
    )(left_env, right_env, mps, psi, coef, sector_sizes, pattern)


def solution(mesh):
    return jax.shard_map(
        shards,
        mesh=mesh,
        in_specs=(
            P("term", None, None, None),
            P("site", "term", None, None, None),
            P("site", None, None, None, None),
            P("site", None, None, None, None),
            P("site", "term", None),
            P(),
            P("term", None),
        ),
        out_specs=P("site", None, "term", None),
        check_vma=False,
    )
```

```python
import functools
import math

import jax
import jax.numpy as jnp
from jax import lax
from jax.experimental import pallas as pl
from jax.experimental.pallas import tpu as pltpu
from jax.sharding import PartitionSpec as P

MESH = pl.DeviceIdType.MESH
FIRST_LAG = 1
HOP_LAG = 1


def halves(x):
    high = x.astype(jnp.bfloat16)
    return high, (x - high.astype(jnp.float32)).astype(jnp.bfloat16)


def product(a, b, left_dim=1, right_dim=0):
    def dot(x, y):
        return lax.dot_general(
            x, y, (((left_dim,), (right_dim,)), ((), ())), preferred_element_type=jnp.float32
        )

    return dot(a[0], b[0]) + (dot(a[0], b[1]) + dot(a[1], b[0]))


def sandwich(block, tensor):
    parts = halves(tensor)
    return product(parts, halves(product(halves(block), parts)), 0, 0)


def kernel(
    sites, terms, unit,
    left, right, mps, psi, coef, sizes, pattern, out,
    e_in, e_out, right_v, mps_v, psi_v, partial, pair_in, up_in, down_in,
    left_sem, right_sem, mps_sem, psi_sem,
    e_send, e_recv, pair_send, pair_recv, z_send, up_recv, down_recv,
):
    nsec, width = e_in.shape[0], e_in.shape[1]
    chips = terms // 2
    rows_owned = nsec * width // terms
    per = rows_owned // unit
    in_sector = width // unit
    site, term = lax.axis_index("site"), lax.axis_index("term")
    chip, core = term // 2, term % 2
    partner = chip * 2 + 1 - core

    def left_copy(q):
        return pltpu.make_async_copy(left.at[0, q], e_in.at[q], left_sem.at[q])

    def right_copy(q):
        return pltpu.make_async_copy(right.at[0, 0, q], right_v.at[q], right_sem.at[q])

    def mps_copy(q):
        return pltpu.make_async_copy(mps.at[0, :, q], mps_v.at[:, q], mps_sem.at[q])

    def psi_copy(q):
        return pltpu.make_async_copy(psi.at[0, :, q], psi_v.at[:, q], psi_sem.at[q])

    @pl.loop(0, nsec)
    def _(q):
        @pl.when(site == 0)
        def _():
            left_copy(q).start()

        mps_copy(q).start()
        psi_copy(q).start()
        right_copy(q).start()

    def e_copy(q):
        return pltpu.make_async_remote_copy(
            src_ref=e_out.at[q], dst_ref=e_in.at[q],
            send_sem=e_send.at[q], recv_sem=e_recv.at[q],
            device_id={"site": jnp.minimum(site + 1, sites - 1)}, device_id_type=MESH,
        )

    def pair_copy(piece, place):
        return pltpu.make_async_remote_copy(
            src_ref=partial.at[piece], dst_ref=pair_in.at[place],
            send_sem=pair_send.at[place], recv_sem=pair_recv.at[place],
            device_id={"term": partner}, device_id_type=MESH,
        )

    def up_copy(piece, place):
        return pltpu.make_async_remote_copy(
            src_ref=partial.at[piece], dst_ref=up_in.at[place],
            send_sem=z_send.at[place], recv_sem=up_recv.at[place],
            device_id={"term": jnp.minimum(term + 2, terms - 2 + core)}, device_id_type=MESH,
        )

    def down_copy(piece, place):
        return pltpu.make_async_remote_copy(
            src_ref=partial.at[piece], dst_ref=down_in.at[place],
            send_sem=z_send.at[place], recv_sem=down_recv.at[place],
            device_id={"term": jnp.maximum(term - 2, core)}, device_id_type=MESH,
        )

    barrier = pltpu.get_barrier_semaphore()
    greet = functools.partial(pl.semaphore_signal, barrier, inc=1, device_id_type=MESH)
    greet(device_id={"term": partner})
    pl.when(site > 0)(lambda: greet(device_id={"site": site - 1}))
    pl.when(site < sites - 1)(lambda: greet(device_id={"site": site + 1}))
    pl.when(chip > 0)(lambda: greet(device_id={"term": term - 2}))
    pl.when(chip < chips - 1)(lambda: greet(device_id={"term": term + 2}))
    bounds = (site > 0, site < sites - 1, chip > 0, chip < chips - 1)
    peers = 1
    for met in bounds:
        peers = peers + jnp.where(met, 1, 0)
    pl.semaphore_wait(barrier, peers)

    rows = lax.broadcasted_iota(jnp.int32, (width, width), 0)
    columns = lax.broadcasted_iota(jnp.int32, (width, width), 1)

    def framed(x, high, wide):
        return jnp.where((rows < high) & (columns < wide), x, 0.0)

    def where_of(piece):
        owner = piece // per
        place = (owner // 2) * per + piece % per
        return owner // 2, owner % 2, place

    right_copy(0).wait()

    def sector(q):
        before, after = jnp.maximum(q - 1, 0), jnp.minimum(q + 1, nsec - 1)
        mps_copy(q).wait()
        pl.when(site == 0)(lambda: left_copy(q).wait())
        pl.when(site > 0)(lambda: e_copy(q).wait_recv())

        size, size_before = sizes[q], sizes[before]
        size_after = jnp.where(q + 1 < nsec, sizes[after], 0)
        there = pattern[0, q].astype(jnp.float32)
        there_after = pattern[0, after].astype(jnp.float32)
        first = jnp.where(site == 0, there, 1.0)
        first_before = jnp.where(site == 0, pattern[0, before].astype(jnp.float32), 1.0)
        same = framed(mps_v[0, q], size, size)
        step = framed(mps_v[1, before], size_before, size)
        here = framed(e_in[q], size, size) * first
        shifted = framed(e_in[before], size_before, size_before) * first_before
        weight = jnp.where(q > 0, coef[0, 0, 1], 0.0)
        e_out[q] = coef[0, 0, 0] * sandwich(here, same) + weight * sandwich(shifted, step)
        pl.when(site < sites - 1)(lambda: e_copy(q).start())

        psi_copy(q).wait()
        pl.when(q + 1 < nsec)(lambda: right_copy(after).wait())
        environ = halves(e_out[q])
        for state, (held, size_r, there_r) in enumerate(
            ((q, size, there), (after, size_after, there_after))
        ):
            psi_block = framed(psi_v[state, q], size, size_r)
            block = framed(right_v[held], size_r, size_r) * there_r
            value = product(environ, halves(psi_block)) * coef[0, 0, 2 + state]
            value = product(halves(value), halves(block), 1, 1)
            for i in range(in_sector):
                partial[q * in_sector + i, state] = value[i * unit:(i + 1) * unit]

        for i in range(in_sector):
            piece = q * in_sector + i
            _, owner_core, place = where_of(piece)
            pl.when(owner_core != core)(lambda: pair_copy(piece, place).start())

    def upward(q):
        for i in range(in_sector):
            piece = q * in_sector + i
            owner_chip, owner_core, place = where_of(piece)

            @pl.when((owner_core == core) & (owner_chip > chip))
            def _():
                pair_copy(piece, place).wait_recv()

                @pl.when(chip == 0)
                def _():
                    partial[piece] = partial[piece] + pair_in[place]

                @pl.when(chip > 0)
                def _():
                    up_copy(piece, place).wait_recv()
                    partial[piece] = (partial[piece] + pair_in[place]) + up_in[place]

                up_copy(piece, place).start()

    def downward(q):
        for i in range(in_sector):
            piece = q * in_sector + i
            owner_chip, owner_core, place = where_of(piece)

            @pl.when((owner_core == core) & (owner_chip < chip))
            def _():
                pair_copy(piece, place).wait_recv()

                @pl.when(chip == chips - 1)
                def _():
                    partial[piece] = partial[piece] + pair_in[place]

                @pl.when(chip < chips - 1)
                def _():
                    down_copy(piece, place).wait_recv()
                    partial[piece] = (partial[piece] + pair_in[place]) + down_in[place]

                down_copy(piece, place).start()

    def ending(q):
        for i in range(in_sector):
            piece = q * in_sector + i
            owner_chip, owner_core, place = where_of(piece)

            @pl.when((owner_core == core) & (owner_chip == chip))
            def _():
                target = pl.ds(pl.multiple_of((piece % per) * unit, unit), unit)
                pair_copy(piece, place).wait_recv()
                out[0, :, target, :] = partial[piece] + pair_in[place]

                @pl.when(chip > 0)
                def _():
                    up_copy(piece, place).wait_recv()
                    out[0, :, target, :] = out[0, :, target, :] + up_in[place]

                @pl.when(chip < chips - 1)
                def _():
                    down_copy(piece, place).wait_recv()
                    out[0, :, target, :] = out[0, :, target, :] + down_in[place]

    from_below, from_above = chip, chips - 1 - chip

    def turn(t, carry):
        for stage, hops in (
            (upward, from_below),
            (downward, from_above),
            (ending, jnp.maximum(from_below, from_above)),
        ):
            q = t - FIRST_LAG - hops * HOP_LAG
            pl.when((q >= 0) & (q < nsec))(lambda: stage(q))
        pl.when(t < nsec)(lambda: sector(t))
        return carry

    lax.fori_loop(0, nsec + FIRST_LAG + (chips - 1) * HOP_LAG, turn, 0)

    @pl.loop(0, nsec)
    def _(q):
        pl.when(site < sites - 1)(lambda: e_copy(q).wait_send())
        for i in range(in_sector):
            piece = q * in_sector + i
            owner_chip, owner_core, place = where_of(piece)
            pl.when(owner_core != core)(lambda: pair_copy(piece, place).wait_send())
            mine = owner_core == core
            pl.when(mine & (owner_chip > chip))(lambda: up_copy(piece, place).wait_send())
            pl.when(mine & (owner_chip < chip))(lambda: down_copy(piece, place).wait_send())


def shards(left_env, right_env, mps, psi, coef, sector_sizes, pattern):
    nsec, width = left_env.shape[1], left_env.shape[-1]
    sites, terms = lax.axis_size("site"), lax.axis_size("term")
    rows_owned = nsec * width // terms
    unit = math.gcd(rows_owned, width)
    pieces = nsec * width // unit
    mine = pieces // 2
    block = (nsec, width, width)
    dma = pltpu.SemaphoreType.DMA
    hbm, smem = pl.BlockSpec(memory_space=pl.ANY), pl.BlockSpec(memory_space=pltpu.SMEM)
    return pl.pallas_call(
        functools.partial(kernel, sites, terms, unit),
        out_shape=jax.ShapeDtypeStruct((1, 2, rows_owned, width), jnp.float32),
        in_specs=[hbm] * 4 + [smem] * 3,
        out_specs=pl.BlockSpec(memory_space=pltpu.VMEM),
        scratch_shapes=[
            pltpu.VMEM(block, jnp.float32),
            pltpu.VMEM(block, jnp.float32),
            pltpu.VMEM(block, jnp.float32),
            pltpu.VMEM((2,) + block, jnp.float32),
            pltpu.VMEM((2,) + block, jnp.float32),
            pltpu.VMEM((pieces, 2, unit, width), jnp.float32),
            pltpu.VMEM((mine, 2, unit, width), jnp.float32),
            pltpu.VMEM((mine, 2, unit, width), jnp.float32),
            pltpu.VMEM((mine, 2, unit, width), jnp.float32),
            dma((nsec,)), dma((nsec,)), dma((nsec,)), dma((nsec,)),
            dma((nsec,)), dma((nsec,)),
            dma((mine,)), dma((mine,)), dma((mine,)), dma((mine,)), dma((mine,)),
        ],
        compiler_params=pltpu.CompilerParams(
            collective_id=0, has_side_effects=True, vmem_limit_bytes=56 * 2**20
        ),
    )(left_env, right_env, mps, psi, coef, sector_sizes, pattern)


def solution(mesh):
    return jax.shard_map(
        shards,
        mesh=mesh,
        in_specs=(
            P("term", None, None, None),
            P("site", "term", None, None, None),
            P("site", None, None, None, None),
            P("site", None, None, None, None),
            P("site", "term", None),
            P(),
            P("term", None),
        ),
        out_specs=P("site", None, "term", None),
        check_vma=False,
    )
```

```python
import functools
import math

import jax
import jax.numpy as jnp
from jax import lax
from jax.experimental import pallas as pl
from jax.experimental.pallas import tpu as pltpu
from jax.sharding import PartitionSpec as P

MESH = pl.DeviceIdType.MESH
FIRST_LAG = 1
HOP_LAG = 1


def halves(x):
    high = x.astype(jnp.bfloat16)
    return high, (x - high.astype(jnp.float32)).astype(jnp.bfloat16)


def joined(parts, first, second, third, axis):
    width = parts.shape[axis] // 2
    pieces = [lax.slice_in_dim(parts, i * width, (i + 1) * width, axis=axis) for i in (0, 1)]
    return jnp.concatenate([pieces[first], pieces[second], pieces[third]], axis=axis)


def beside(x, axis=1):
    return jnp.concatenate(halves(x), axis=axis)


def dot(x, y, right_dim):
    return lax.dot_general(
        x, y, (((1,), (right_dim,)), ((), ())), preferred_element_type=jnp.float32
    )


def as_left(parts):
    return joined(parts, 0, 1, 0, 1)


def as_right(parts, axis):
    return joined(parts, 0, 0, 1, axis)


def kernel(
    sites, terms, unit,
    left, right, mps, psi, coef, sizes, pattern, out,
    e_in, e_out, right_v, mps_v, psi_v, partial, pair_in, up_in, down_in,
    environs, tensors, states, rights,
    left_sem, right_sem, mps_sem, psi_sem,
    e_send, e_recv, pair_send, pair_recv, z_send, up_recv, down_recv,
):
    nsec, width = e_in.shape[0], e_in.shape[1]
    chips = terms // 2
    rows_owned = nsec * width // terms
    per = rows_owned // unit
    in_sector = width // unit
    site, term = lax.axis_index("site"), lax.axis_index("term")
    chip, core = term // 2, term % 2
    partner = chip * 2 + 1 - core

    def left_copy(q):
        return pltpu.make_async_copy(left.at[0, q], e_in.at[q], left_sem.at[q])

    def right_copy(q):
        return pltpu.make_async_copy(right.at[0, 0, q], right_v.at[q], right_sem.at[q])

    def mps_copy(q):
        return pltpu.make_async_copy(mps.at[0, :, q], mps_v.at[:, q], mps_sem.at[q])

    def psi_copy(q):
        return pltpu.make_async_copy(psi.at[0, :, q], psi_v.at[:, q], psi_sem.at[q])

    @pl.loop(0, nsec)
    def _(q):
        @pl.when(site == 0)
        def _():
            left_copy(q).start()

        mps_copy(q).start()
        psi_copy(q).start()
        right_copy(q).start()

    def e_copy(q):
        return pltpu.make_async_remote_copy(
            src_ref=e_out.at[q], dst_ref=e_in.at[q],
            send_sem=e_send.at[q], recv_sem=e_recv.at[q],
            device_id={"site": jnp.minimum(site + 1, sites - 1)}, device_id_type=MESH,
        )

    def pair_copy(piece, place):
        return pltpu.make_async_remote_copy(
            src_ref=partial.at[piece], dst_ref=pair_in.at[place],
            send_sem=pair_send.at[place], recv_sem=pair_recv.at[place],
            device_id={"term": partner}, device_id_type=MESH,
        )

    def up_copy(piece, place):
        return pltpu.make_async_remote_copy(
            src_ref=partial.at[piece], dst_ref=up_in.at[place],
            send_sem=z_send.at[place], recv_sem=up_recv.at[place],
            device_id={"term": jnp.minimum(term + 2, terms - 2 + core)}, device_id_type=MESH,
        )

    def down_copy(piece, place):
        return pltpu.make_async_remote_copy(
            src_ref=partial.at[piece], dst_ref=down_in.at[place],
            send_sem=z_send.at[place], recv_sem=down_recv.at[place],
            device_id={"term": jnp.maximum(term - 2, core)}, device_id_type=MESH,
        )

    barrier = pltpu.get_barrier_semaphore()
    greet = functools.partial(pl.semaphore_signal, barrier, inc=1, device_id_type=MESH)
    greet(device_id={"term": partner})
    pl.when(site > 0)(lambda: greet(device_id={"site": site - 1}))
    pl.when(site < sites - 1)(lambda: greet(device_id={"site": site + 1}))
    pl.when(chip > 0)(lambda: greet(device_id={"term": term - 2}))
    pl.when(chip < chips - 1)(lambda: greet(device_id={"term": term + 2}))
    bounds = (site > 0, site < sites - 1, chip > 0, chip < chips - 1)
    peers = 1
    for met in bounds:
        peers = peers + jnp.where(met, 1, 0)
    pl.semaphore_wait(barrier, peers)

    rows = lax.broadcasted_iota(jnp.int32, (width, width), 0)
    columns = lax.broadcasted_iota(jnp.int32, (width, width), 1)

    def framed(x, high, wide):
        return jnp.where((rows < high) & (columns < wide), x, 0.0)

    def where_of(piece):
        owner = piece // per
        place = (owner // 2) * per + piece % per
        return owner // 2, owner % 2, place

    def prepare_right(h):
        held = jnp.minimum(h, nsec - 1)
        size = jnp.where(h < nsec, sizes[held], 0)
        there = pattern[0, held].astype(jnp.float32)
        rights[h % 3] = beside(framed(right_v[held], size, size) * there)

    def prepare_tensors(h):
        q = jnp.minimum(h, nsec - 1)
        before, after = jnp.maximum(q - 1, 0), jnp.minimum(q + 1, nsec - 1)
        size, size_before = sizes[q], sizes[before]
        size_after = jnp.where(q + 1 < nsec, sizes[after], 0)
        tensors[h % 2, 0] = beside(framed(mps_v[0, q], size, size).T)
        tensors[h % 2, 1] = beside(framed(mps_v[1, before], size_before, size).T)
        states[h % 2] = jnp.concatenate(
            [
                beside(framed(psi_v[0, q], size, size), 0),
                beside(framed(psi_v[1, q], size, size_after), 0),
            ],
            axis=1,
        )

    environs[1] = jnp.zeros((width, 2 * width), jnp.bfloat16)
    mps_copy(0).wait()
    psi_copy(0).wait()
    right_copy(0).wait()
    right_copy(1).wait()
    prepare_tensors(0)
    prepare_right(0)
    prepare_right(1)

    def update(q):
        pl.when(site == 0)(lambda: left_copy(q).wait())
        pl.when(site > 0)(lambda: e_copy(q).wait_recv())
        size = sizes[q]
        first = jnp.where(site == 0, pattern[0, q].astype(jnp.float32), 1.0)
        environs[q % 2] = beside(framed(e_in[q], size, size) * first)
        weight = jnp.where(q > 0, coef[0, 0, 1], 0.0)
        same, step = tensors[q % 2, 0], tensors[q % 2, 1]
        here = dot(as_left(environs[q % 2]), as_right(same, 1), 1) * coef[0, 0, 0]
        shifted = dot(as_left(environs[(q + 1) % 2]), as_right(step, 1), 1) * weight
        e_out[q] = dot(
            jnp.concatenate([as_left(same), as_left(step)], axis=1),
            jnp.concatenate([as_right(beside(here, 0), 0), as_right(beside(shifted, 0), 0)], axis=0),
            0,
        )
        pl.when(site < sites - 1)(lambda: e_copy(q).start())

    def apply(q):
        @pl.when(q + 1 < nsec)
        def _():
            mps_copy(q + 1).wait()
            psi_copy(q + 1).wait()

        pl.when(q + 2 < nsec)(lambda: right_copy(q + 2).wait())
        both = dot(as_left(beside(e_out[q])), as_right(states[q % 2], 0), 0)
        for state in (0, 1):
            value = both[:, state * width:(state + 1) * width] * coef[0, 0, 2 + state]
            value = dot(as_left(beside(value)), as_right(rights[(q + state) % 3], 1), 1)
            for i in range(in_sector):
                partial[q * in_sector + i, state] = value[i * unit:(i + 1) * unit]
        prepare_tensors(q + 1)
        prepare_right(q + 2)

        for i in range(in_sector):
            piece = q * in_sector + i
            _, owner_core, place = where_of(piece)
            pl.when(owner_core != core)(lambda: pair_copy(piece, place).start())

    def upward(q):
        for i in range(in_sector):
            piece = q * in_sector + i
            owner_chip, owner_core, place = where_of(piece)

            @pl.when((owner_core == core) & (owner_chip > chip))
            def _():
                pair_copy(piece, place).wait_recv()

                @pl.when(chip == 0)
                def _():
                    partial[piece] = partial[piece] + pair_in[place]

                @pl.when(chip > 0)
                def _():
                    up_copy(piece, place).wait_recv()
                    partial[piece] = (partial[piece] + pair_in[place]) + up_in[place]

                up_copy(piece, place).start()

    def downward(q):
        for i in range(in_sector):
            piece = q * in_sector + i
            owner_chip, owner_core, place = where_of(piece)

            @pl.when((owner_core == core) & (owner_chip < chip))
            def _():
                pair_copy(piece, place).wait_recv()

                @pl.when(chip == chips - 1)
                def _():
                    partial[piece] = partial[piece] + pair_in[place]

                @pl.when(chip < chips - 1)
                def _():
                    down_copy(piece, place).wait_recv()
                    partial[piece] = (partial[piece] + pair_in[place]) + down_in[place]

                down_copy(piece, place).start()

    def ending(q):
        for i in range(in_sector):
            piece = q * in_sector + i
            owner_chip, owner_core, place = where_of(piece)

            @pl.when((owner_core == core) & (owner_chip == chip))
            def _():
                target = pl.ds(pl.multiple_of((piece % per) * unit, unit), unit)
                pair_copy(piece, place).wait_recv()
                out[0, :, target, :] = partial[piece] + pair_in[place]

                @pl.when(chip > 0)
                def _():
                    up_copy(piece, place).wait_recv()
                    out[0, :, target, :] = out[0, :, target, :] + up_in[place]

                @pl.when(chip < chips - 1)
                def _():
                    down_copy(piece, place).wait_recv()
                    out[0, :, target, :] = out[0, :, target, :] + down_in[place]

    from_below, from_above = chip, chips - 1 - chip

    def turn(t, carry):
        pl.when(t < nsec)(lambda: update(t))
        for stage, hops in (
            (upward, from_below),
            (downward, from_above),
            (ending, jnp.maximum(from_below, from_above)),
        ):
            q = t - FIRST_LAG - hops * HOP_LAG
            pl.when((q >= 0) & (q < nsec))(lambda: stage(q))
        pl.when(t < nsec)(lambda: apply(t))
        return carry

    lax.fori_loop(0, nsec + FIRST_LAG + (chips - 1) * HOP_LAG, turn, 0)

    @pl.loop(0, nsec)
    def _(q):
        pl.when(site < sites - 1)(lambda: e_copy(q).wait_send())
        for i in range(in_sector):
            piece = q * in_sector + i
            owner_chip, owner_core, place = where_of(piece)
            pl.when(owner_core != core)(lambda: pair_copy(piece, place).wait_send())
            mine = owner_core == core
            pl.when(mine & (owner_chip > chip))(lambda: up_copy(piece, place).wait_send())
            pl.when(mine & (owner_chip < chip))(lambda: down_copy(piece, place).wait_send())


def shards(left_env, right_env, mps, psi, coef, sector_sizes, pattern):
    nsec, width = left_env.shape[1], left_env.shape[-1]
    sites, terms = lax.axis_size("site"), lax.axis_size("term")
    rows_owned = nsec * width // terms
    unit = math.gcd(rows_owned, width)
    pieces = nsec * width // unit
    mine = pieces // 2
    block = (nsec, width, width)
    dma = pltpu.SemaphoreType.DMA
    hbm, smem = pl.BlockSpec(memory_space=pl.ANY), pl.BlockSpec(memory_space=pltpu.SMEM)
    return pl.pallas_call(
        functools.partial(kernel, sites, terms, unit),
        out_shape=jax.ShapeDtypeStruct((1, 2, rows_owned, width), jnp.float32),
        in_specs=[hbm] * 4 + [smem] * 3,
        out_specs=pl.BlockSpec(memory_space=pltpu.VMEM),
        scratch_shapes=[
            pltpu.VMEM(block, jnp.float32),
            pltpu.VMEM(block, jnp.float32),
            pltpu.VMEM(block, jnp.float32),
            pltpu.VMEM((2,) + block, jnp.float32),
            pltpu.VMEM((2,) + block, jnp.float32),
            pltpu.VMEM((pieces, 2, unit, width), jnp.float32),
            pltpu.VMEM((mine, 2, unit, width), jnp.float32),
            pltpu.VMEM((mine, 2, unit, width), jnp.float32),
            pltpu.VMEM((mine, 2, unit, width), jnp.float32),
            pltpu.VMEM((2, width, 2 * width), jnp.bfloat16),
            pltpu.VMEM((2, 2, width, 2 * width), jnp.bfloat16),
            pltpu.VMEM((2, 2 * width, 2 * width), jnp.bfloat16),
            pltpu.VMEM((3, width, 2 * width), jnp.bfloat16),
            dma((nsec,)), dma((nsec,)), dma((nsec,)), dma((nsec,)),
            dma((nsec,)), dma((nsec,)),
            dma((mine,)), dma((mine,)), dma((mine,)), dma((mine,)), dma((mine,)),
        ],
        compiler_params=pltpu.CompilerParams(
            collective_id=0, has_side_effects=True, vmem_limit_bytes=56 * 2**20
        ),
    )(left_env, right_env, mps, psi, coef, sector_sizes, pattern)


def solution(mesh):
    return jax.shard_map(
        shards,
        mesh=mesh,
        in_specs=(
            P("term", None, None, None),
            P("site", "term", None, None, None),
            P("site", None, None, None, None),
            P("site", None, None, None, None),
            P("site", "term", None),
            P(),
            P("term", None),
        ),
        out_specs=P("site", None, "term", None),
        check_vma=False,
    )
```

```python
import functools
import math

import jax
import jax.numpy as jnp
from jax import lax
from jax.experimental import pallas as pl
from jax.experimental.pallas import tpu as pltpu
from jax.sharding import PartitionSpec as P

MESH = pl.DeviceIdType.MESH
FIRST_LAG = 1
HOP_LAG = 1


def halves(x):
    high = x.astype(jnp.bfloat16)
    return high, (x - high.astype(jnp.float32)).astype(jnp.bfloat16)


def joined(parts, first, second, third, axis):
    width = parts.shape[axis] // 2
    pieces = [lax.slice_in_dim(parts, i * width, (i + 1) * width, axis=axis) for i in (0, 1)]
    return jnp.concatenate([pieces[first], pieces[second], pieces[third]], axis=axis)


def beside(x, axis=1):
    return jnp.concatenate(halves(x), axis=axis)


def dot(x, y, right_dim):
    return lax.dot_general(
        x, y, (((1,), (right_dim,)), ((), ())), preferred_element_type=jnp.float32
    )


def as_left(parts):
    return joined(parts, 0, 1, 0, 1)


def as_right(parts, axis):
    return joined(parts, 0, 0, 1, axis)


def kernel(
    sites, terms, unit,
    left, right, mps, psi, coef, sizes, pattern, out,
    e_in, e_out, right_v, mps_v, psi_v, partial, pair_in, up_in, down_in, last_in,
    environs, tensors, states, rights,
    left_sem, right_sem, mps_sem, psi_sem,
    e_send, e_recv, pair_send, pair_recv, z_send, up_recv, down_recv,
    last_send, last_recv,
):
    nsec, width = e_in.shape[0], e_in.shape[1]
    chips = terms // 2
    rows_owned = nsec * width // terms
    per = rows_owned // unit
    in_sector = width // unit
    site, term = lax.axis_index("site"), lax.axis_index("term")
    chip, core = term // 2, term % 2
    partner = chip * 2 + 1 - core

    def left_copy(q):
        return pltpu.make_async_copy(left.at[0, q], e_in.at[q], left_sem.at[q])

    def right_copy(q):
        return pltpu.make_async_copy(right.at[0, 0, q], right_v.at[q], right_sem.at[q])

    def mps_copy(q):
        return pltpu.make_async_copy(mps.at[0, :, q], mps_v.at[:, q], mps_sem.at[q])

    def psi_copy(q):
        return pltpu.make_async_copy(psi.at[0, :, q], psi_v.at[:, q], psi_sem.at[q])

    @pl.loop(0, nsec)
    def _(q):
        @pl.when(site == 0)
        def _():
            left_copy(q).start()

        mps_copy(q).start()
        psi_copy(q).start()
        right_copy(q).start()

    def e_copy(q):
        return pltpu.make_async_remote_copy(
            src_ref=e_out.at[q], dst_ref=e_in.at[q],
            send_sem=e_send.at[q], recv_sem=e_recv.at[q],
            device_id={"site": jnp.minimum(site + 1, sites - 1)}, device_id_type=MESH,
        )

    def pair_copy(piece):
        return pltpu.make_async_remote_copy(
            src_ref=partial.at[piece, 1 - core], dst_ref=pair_in.at[piece],
            send_sem=pair_send.at[piece], recv_sem=pair_recv.at[piece],
            device_id={"term": partner}, device_id_type=MESH,
        )

    def up_copy(piece):
        return pltpu.make_async_remote_copy(
            src_ref=partial.at[piece, core], dst_ref=up_in.at[piece],
            send_sem=z_send.at[piece], recv_sem=up_recv.at[piece],
            device_id={"term": jnp.minimum(term + 2, terms - 2 + core)}, device_id_type=MESH,
        )

    def down_copy(piece):
        return pltpu.make_async_remote_copy(
            src_ref=partial.at[piece, core], dst_ref=down_in.at[piece],
            send_sem=z_send.at[piece], recv_sem=down_recv.at[piece],
            device_id={"term": jnp.maximum(term - 2, core)}, device_id_type=MESH,
        )

    def last_copy(piece):
        return pltpu.make_async_remote_copy(
            src_ref=partial.at[piece, core], dst_ref=last_in.at[piece % per],
            send_sem=last_send.at[piece % per], recv_sem=last_recv.at[piece % per],
            device_id={"term": partner}, device_id_type=MESH,
        )

    barrier = pltpu.get_barrier_semaphore()
    greet = functools.partial(pl.semaphore_signal, barrier, inc=1, device_id_type=MESH)
    greet(device_id={"term": partner})
    pl.when(site > 0)(lambda: greet(device_id={"site": site - 1}))
    pl.when(site < sites - 1)(lambda: greet(device_id={"site": site + 1}))
    pl.when(chip > 0)(lambda: greet(device_id={"term": term - 2}))
    pl.when(chip < chips - 1)(lambda: greet(device_id={"term": term + 2}))
    bounds = (site > 0, site < sites - 1, chip > 0, chip < chips - 1)
    peers = 1
    for met in bounds:
        peers = peers + jnp.where(met, 1, 0)
    pl.semaphore_wait(barrier, peers)

    rows = lax.broadcasted_iota(jnp.int32, (width, width), 0)
    columns = lax.broadcasted_iota(jnp.int32, (width, width), 1)

    def framed(x, high, wide):
        return jnp.where((rows < high) & (columns < wide), x, 0.0)

    def prepare_right(h):
        held = jnp.minimum(h, nsec - 1)
        size = jnp.where(h < nsec, sizes[held], 0)
        there = pattern[0, held].astype(jnp.float32)
        rights[h % 3] = beside(framed(right_v[held], size, size) * there)

    def prepare_tensors(h):
        q = jnp.minimum(h, nsec - 1)
        before, after = jnp.maximum(q - 1, 0), jnp.minimum(q + 1, nsec - 1)
        size, size_before = sizes[q], sizes[before]
        size_after = jnp.where(q + 1 < nsec, sizes[after], 0)
        tensors[h % 2, 0] = beside(framed(mps_v[0, q], size, size).T)
        tensors[h % 2, 1] = beside(framed(mps_v[1, before], size_before, size).T)
        states[h % 2] = jnp.concatenate(
            [
                beside(framed(psi_v[0, q], size, size), 0),
                beside(framed(psi_v[1, q], size, size_after), 0),
            ],
            axis=1,
        )

    environs[1] = jnp.zeros((width, 2 * width), jnp.bfloat16)
    mps_copy(0).wait()
    psi_copy(0).wait()
    right_copy(0).wait()
    right_copy(1).wait()
    prepare_tensors(0)
    prepare_right(0)
    prepare_right(1)

    def update(q):
        pl.when(site == 0)(lambda: left_copy(q).wait())
        pl.when(site > 0)(lambda: e_copy(q).wait_recv())
        size = sizes[q]
        first = jnp.where(site == 0, pattern[0, q].astype(jnp.float32), 1.0)
        environs[q % 2] = beside(framed(e_in[q], size, size) * first)
        weight = jnp.where(q > 0, coef[0, 0, 1], 0.0)
        same, step = tensors[q % 2, 0], tensors[q % 2, 1]
        here = dot(as_left(environs[q % 2]), as_right(same, 1), 1) * coef[0, 0, 0]
        shifted = dot(as_left(environs[(q + 1) % 2]), as_right(step, 1), 1) * weight
        e_out[q] = dot(
            jnp.concatenate([as_left(same), as_left(step)], axis=1),
            jnp.concatenate([as_right(beside(here, 0), 0), as_right(beside(shifted, 0), 0)], axis=0),
            0,
        )
        pl.when(site < sites - 1)(lambda: e_copy(q).start())

    def apply(q):
        @pl.when(q + 1 < nsec)
        def _():
            mps_copy(q + 1).wait()
            psi_copy(q + 1).wait()

        pl.when(q + 2 < nsec)(lambda: right_copy(q + 2).wait())
        both = dot(as_left(beside(e_out[q])), as_right(states[q % 2], 0), 0)
        for state in (0, 1):
            value = both[:, state * width:(state + 1) * width] * coef[0, 0, 2 + state]
            value = dot(as_left(beside(value)), as_right(rights[(q + state) % 3], 1), 1)
            for i in range(in_sector):
                partial[q * in_sector + i, state] = value[i * unit:(i + 1) * unit]
        prepare_tensors(q + 1)
        prepare_right(q + 2)

        for i in range(in_sector):
            pair_copy(q * in_sector + i).start()

    def forward(q, chosen, first, arrived, copy):
        for i in range(in_sector):
            piece = q * in_sector + i
            owner_chip = piece // per // 2

            @pl.when(chosen(owner_chip))
            def _():
                pair_copy(piece).wait_recv()

                @pl.when(first)
                def _():
                    partial[piece, core] = partial[piece, core] + pair_in[piece]

                @pl.when(jnp.logical_not(first))
                def _():
                    copy(piece).wait_recv()
                    partial[piece, core] = (partial[piece, core] + pair_in[piece]) + arrived[piece]

                copy(piece).start()

    def upward(q):
        forward(q, lambda owner_chip: owner_chip > chip, chip == 0, up_in, up_copy)

    def downward(q):
        forward(q, lambda owner_chip: owner_chip < chip, chip == chips - 1, down_in, down_copy)

    def ending(q):
        for i in range(in_sector):
            piece = q * in_sector + i
            owner = piece // per

            @pl.when(owner // 2 == chip)
            def _():
                pair_copy(piece).wait_recv()
                partial[piece, core] = partial[piece, core] + pair_in[piece]

                @pl.when(chip > 0)
                def _():
                    up_copy(piece).wait_recv()
                    partial[piece, core] = partial[piece, core] + up_in[piece]

                @pl.when(chip < chips - 1)
                def _():
                    down_copy(piece).wait_recv()
                    partial[piece, core] = partial[piece, core] + down_in[piece]

                @pl.when(owner % 2 == core)
                def _():
                    target = pl.ds(pl.multiple_of((piece % per) * unit, unit), unit)
                    out[0, core, target, :] = partial[piece, core]

                pl.when(owner % 2 != core)(lambda: last_copy(piece).start())

    from_below, from_above = chip, chips - 1 - chip

    def turn(t, carry):
        @pl.when(t < nsec)
        def _():
            update(t)
            apply(t)

        for stage, hops in (
            (upward, from_below),
            (downward, from_above),
            (ending, jnp.maximum(from_below, from_above)),
        ):
            q = t - FIRST_LAG - hops * HOP_LAG
            pl.when((q >= 0) & (q < nsec))(lambda: stage(q))
        return carry

    lax.fori_loop(0, nsec + FIRST_LAG + (chips - 1) * HOP_LAG, turn, 0)

    @pl.loop(0, nsec)
    def _(q):
        pl.when(site < sites - 1)(lambda: e_copy(q).wait_send())
        for i in range(in_sector):
            piece = q * in_sector + i
            owner_chip = piece // per // 2
            pair_copy(piece).wait_send()
            pl.when(owner_chip > chip)(lambda: up_copy(piece).wait_send())
            pl.when(owner_chip < chip)(lambda: down_copy(piece).wait_send())

    @pl.loop(0, per)
    def _(i):
        last_copy(i).wait()
        target = pl.ds(pl.multiple_of(i * unit, unit), unit)
        out[0, 1 - core, target, :] = last_in[i]


def shards(left_env, right_env, mps, psi, coef, sector_sizes, pattern):
    nsec, width = left_env.shape[1], left_env.shape[-1]
    sites, terms = lax.axis_size("site"), lax.axis_size("term")
    rows_owned = nsec * width // terms
    unit = math.gcd(rows_owned, width)
    pieces = nsec * width // unit
    per = rows_owned // unit
    block = (nsec, width, width)
    dma = pltpu.SemaphoreType.DMA
    hbm, smem = pl.BlockSpec(memory_space=pl.ANY), pl.BlockSpec(memory_space=pltpu.SMEM)
    return pl.pallas_call(
        functools.partial(kernel, sites, terms, unit),
        out_shape=jax.ShapeDtypeStruct((1, 2, rows_owned, width), jnp.float32),
        in_specs=[hbm] * 4 + [smem] * 3,
        out_specs=pl.BlockSpec(memory_space=pltpu.VMEM),
        scratch_shapes=[
            pltpu.VMEM(block, jnp.float32),
            pltpu.VMEM(block, jnp.float32),
            pltpu.VMEM(block, jnp.float32),
            pltpu.VMEM((2,) + block, jnp.float32),
            pltpu.VMEM((2,) + block, jnp.float32),
            pltpu.VMEM((pieces, 2, unit, width), jnp.float32),
            pltpu.VMEM((pieces, unit, width), jnp.float32),
            pltpu.VMEM((pieces, unit, width), jnp.float32),
            pltpu.VMEM((pieces, unit, width), jnp.float32),
            pltpu.VMEM((per, unit, width), jnp.float32),
            pltpu.VMEM((2, width, 2 * width), jnp.bfloat16),
            pltpu.VMEM((2, 2, width, 2 * width), jnp.bfloat16),
            pltpu.VMEM((2, 2 * width, 2 * width), jnp.bfloat16),
            pltpu.VMEM((3, width, 2 * width), jnp.bfloat16),
            dma((nsec,)), dma((nsec,)), dma((nsec,)), dma((nsec,)),
            dma((nsec,)), dma((nsec,)),
            dma((pieces,)), dma((pieces,)), dma((pieces,)), dma((pieces,)), dma((pieces,)),
            dma((per,)), dma((per,)),
        ],
        compiler_params=pltpu.CompilerParams(
            collective_id=0, has_side_effects=True, vmem_limit_bytes=56 * 2**20
        ),
    )(left_env, right_env, mps, psi, coef, sector_sizes, pattern)


def solution(mesh):
    return jax.shard_map(
        shards,
        mesh=mesh,
        in_specs=(
            P("term", None, None, None),
            P("site", "term", None, None, None),
            P("site", None, None, None, None),
            P("site", None, None, None, None),
            P("site", "term", None),
            P(),
            P("term", None),
        ),
        out_specs=P("site", None, "term", None),
        check_vma=False,
    )
```

```python
import functools
import math

import jax
import jax.numpy as jnp
from jax import lax
from jax.experimental import pallas as pl
from jax.experimental.pallas import tpu as pltpu
from jax.sharding import PartitionSpec as P

MESH = pl.DeviceIdType.MESH
FIRST_LAG = 1
HOP_LAG = 1
LEAD = 4


def halves(x):
    high = x.astype(jnp.bfloat16)
    return high, (x - high.astype(jnp.float32)).astype(jnp.bfloat16)


def joined(parts, first, second, third, axis):
    width = parts.shape[axis] // 2
    pieces = [lax.slice_in_dim(parts, i * width, (i + 1) * width, axis=axis) for i in (0, 1)]
    return jnp.concatenate([pieces[first], pieces[second], pieces[third]], axis=axis)


def beside(x, axis=1):
    return jnp.concatenate(halves(x), axis=axis)


def dot(x, y, right_dim):
    return lax.dot_general(
        x, y, (((1,), (right_dim,)), ((), ())), preferred_element_type=jnp.float32
    )


def as_left(parts):
    return joined(parts, 0, 1, 0, 1)


def as_right(parts, axis):
    return joined(parts, 0, 0, 1, axis)


def kernel(
    sites, terms, unit,
    left, right, mps, psi, coef, sizes, pattern, out,
    e_in, e_out, right_v, mps_v, psi_v, partial, pair_in, up_in, down_in, last_in,
    environs, tensors, states, rights,
    mps_in, middles, earlier, coef_out, coef_in,
    left_sem, right_sem, mps_sem, psi_sem,
    e_send, e_recv, pair_send, pair_recv, z_send, up_recv, down_recv,
    last_send, last_recv,
    e_send_far, tensor_send, tensor_recv, swap_send, swap_recv, coef_sem,
):
    nsec, width = e_in.shape[0], e_in.shape[1]
    chips = terms // 2
    rows_owned = nsec * width // terms
    per = rows_owned // unit
    in_sector = width // unit
    site, term = lax.axis_index("site"), lax.axis_index("term")
    chip, core = term // 2, term % 2
    partner = chip * 2 + 1 - core
    odd = site % 2 == 1
    even = site % 2 == 0
    leading = even & (site < sites - 1)

    def left_copy(q):
        return pltpu.make_async_copy(left.at[0, q], e_in.at[q], left_sem.at[q])

    def right_copy(q):
        return pltpu.make_async_copy(right.at[0, 0, q], right_v.at[q], right_sem.at[q])

    def mps_copy(q):
        return pltpu.make_async_copy(mps.at[0, :, q], mps_v.at[:, q], mps_sem.at[q])

    def psi_copy(q):
        return pltpu.make_async_copy(psi.at[0, :, q], psi_v.at[:, q], psi_sem.at[q])

    @pl.loop(0, nsec)
    def _(q):
        pl.when(site < 2)(lambda: left_copy(q).start())

        mps_copy(q).start()
        psi_copy(q).start()
        right_copy(q).start()

    def e_copy(q, by=1):
        return pltpu.make_async_remote_copy(
            src_ref=e_out.at[q], dst_ref=e_in.at[q],
            send_sem=(e_send if by == 1 else e_send_far).at[q], recv_sem=e_recv.at[q],
            device_id={"site": jnp.minimum(site + by, sites - 1)}, device_id_type=MESH,
        )

    def tensor_copy(q):
        return pltpu.make_async_remote_copy(
            src_ref=mps.at[0, core, q], dst_ref=mps_in.at[core, q],
            send_sem=tensor_send.at[q], recv_sem=tensor_recv.at[q],
            device_id={"site": jnp.minimum(site + 1, sites - 1)}, device_id_type=MESH,
        )

    def swap_copy(q, state):
        return pltpu.make_async_remote_copy(
            src_ref=mps_in.at[state, q], dst_ref=mps_in.at[state, q],
            send_sem=swap_send.at[q], recv_sem=swap_recv.at[q],
            device_id={"term": partner}, device_id_type=MESH,
        )

    def coef_copy():
        return pltpu.make_async_remote_copy(
            src_ref=coef_out, dst_ref=coef_in,
            send_sem=coef_sem.at[0], recv_sem=coef_sem.at[1],
            device_id={"site": jnp.minimum(site + 1, sites - 1)}, device_id_type=MESH,
        )

    def pair_copy(piece):
        return pltpu.make_async_remote_copy(
            src_ref=partial.at[piece, 1 - core], dst_ref=pair_in.at[piece],
            send_sem=pair_send.at[piece], recv_sem=pair_recv.at[piece],
            device_id={"term": partner}, device_id_type=MESH,
        )

    def up_copy(piece):
        return pltpu.make_async_remote_copy(
            src_ref=partial.at[piece, core], dst_ref=up_in.at[piece],
            send_sem=z_send.at[piece], recv_sem=up_recv.at[piece],
            device_id={"term": jnp.minimum(term + 2, terms - 2 + core)}, device_id_type=MESH,
        )

    def down_copy(piece):
        return pltpu.make_async_remote_copy(
            src_ref=partial.at[piece, core], dst_ref=down_in.at[piece],
            send_sem=z_send.at[piece], recv_sem=down_recv.at[piece],
            device_id={"term": jnp.maximum(term - 2, core)}, device_id_type=MESH,
        )

    def last_copy(piece):
        return pltpu.make_async_remote_copy(
            src_ref=partial.at[piece, core], dst_ref=last_in.at[piece % per],
            send_sem=last_send.at[piece % per], recv_sem=last_recv.at[piece % per],
            device_id={"term": partner}, device_id_type=MESH,
        )

    barrier = pltpu.get_barrier_semaphore()
    greet = functools.partial(pl.semaphore_signal, barrier, inc=1, device_id_type=MESH)
    greet(device_id={"term": partner})
    pl.when(site > 0)(lambda: greet(device_id={"site": site - 1}))
    pl.when(site < sites - 1)(lambda: greet(device_id={"site": site + 1}))
    far_below, far_above = odd & (site > 1), odd & (site + 2 < sites)
    pl.when(far_below)(lambda: greet(device_id={"site": site - 2}))
    pl.when(far_above)(lambda: greet(device_id={"site": site + 2}))
    pl.when(chip > 0)(lambda: greet(device_id={"term": term - 2}))
    pl.when(chip < chips - 1)(lambda: greet(device_id={"term": term + 2}))
    bounds = (site > 0, site < sites - 1, far_below, far_above, chip > 0, chip < chips - 1)
    peers = 1
    for met in bounds:
        peers = peers + jnp.where(met, 1, 0)
    pl.semaphore_wait(barrier, peers)

    lanes = lax.broadcasted_iota(jnp.int32, coef_out.shape, 1)
    coef_out[...] = jnp.where(lanes == 0, coef[0, 0, 0], coef[0, 0, 1])

    @pl.when(leading)
    def _():
        coef_copy().start()
        pl.loop(0, min(LEAD, nsec))(lambda q: tensor_copy(q).start())

    rows = lax.broadcasted_iota(jnp.int32, (width, width), 0)
    columns = lax.broadcasted_iota(jnp.int32, (width, width), 1)

    def framed(x, high, wide):
        return jnp.where((rows < high) & (columns < wide), x, 0.0)

    def prepare_right(h):
        held = jnp.minimum(h, nsec - 1)
        size = jnp.where(h < nsec, sizes[held], 0)
        there = pattern[0, held].astype(jnp.float32)
        rights[h % 3] = beside(framed(right_v[held], size, size) * there)

    def prepare_tensors(h):
        q = jnp.minimum(h, nsec - 1)
        before, after = jnp.maximum(q - 1, 0), jnp.minimum(q + 1, nsec - 1)
        size, size_before = sizes[q], sizes[before]
        size_after = jnp.where(q + 1 < nsec, sizes[after], 0)
        tensors[h % 2, 0] = beside(framed(mps_v[0, q], size, size).T)
        tensors[h % 2, 1] = beside(framed(mps_v[1, before], size_before, size).T)
        states[h % 2] = jnp.concatenate(
            [
                beside(framed(psi_v[0, q], size, size), 0),
                beside(framed(psi_v[1, q], size, size_after), 0),
            ],
            axis=1,
        )

    environs[1] = jnp.zeros((width, 2 * width), jnp.bfloat16)
    middles[1] = jnp.zeros((width, 2 * width), jnp.bfloat16)
    mps_copy(0).wait()
    psi_copy(0).wait()
    right_copy(0).wait()
    right_copy(1).wait()
    prepare_tensors(0)
    prepare_right(0)
    prepare_right(1)

    def receive(q):
        tensor_copy(q).wait_recv()
        swap_copy(q, core).start()

    @pl.when(odd)
    def _():
        coef_copy().wait_recv()
        receive(0)

    def advanced(blocks, q, same, step, weights):
        here = dot(as_left(blocks[q % 2]), as_right(same, 1), 1) * weights[0]
        shifted = dot(as_left(blocks[(q + 1) % 2]), as_right(step, 1), 1) * weights[1]
        return dot(
            jnp.concatenate([as_left(same), as_left(step)], axis=1),
            jnp.concatenate([as_right(beside(here, 0), 0), as_right(beside(shifted, 0), 0)], axis=0),
            0,
        )

    def update(q):
        before = jnp.maximum(q - 1, 0)
        pl.when(site < 2)(lambda: left_copy(q).wait())
        pl.when(site > 1)(lambda: e_copy(q).wait_recv())
        size, size_before = sizes[q], sizes[before]
        first = jnp.where(site < 2, pattern[0, q].astype(jnp.float32), 1.0)
        below = jnp.where(q > 0, 1.0, 0.0)
        weights = coef[0, 0, 0], coef[0, 0, 1] * below

        @pl.when(odd)
        def _():
            swap_copy(q, 1 - core).wait_recv()
            earlier[0] = beside(framed(mps_in[0, q], size, size).T)
            earlier[1] = beside(framed(mps_in[1, before], size_before, size).T)
            environs[q % 2] = beside(framed(e_in[q], size, size) * first)
            weights_in = coef_in[0:1, 0:1], coef_in[0:1, 1:2] * below
            middle = advanced(environs, q, earlier[0], earlier[1], weights_in)
            middles[q % 2] = beside(middle)
            e_out[q] = advanced(middles, q, tensors[q % 2, 0], tensors[q % 2, 1], weights)
            pl.when(site + 1 < sites)(lambda: e_copy(q).start())
            pl.when(site + 2 < sites)(lambda: e_copy(q, 2).start())

        @pl.when(even)
        def _():
            environs[q % 2] = beside(framed(e_in[q], size, size) * first)
            e_out[q] = advanced(environs, q, tensors[q % 2, 0], tensors[q % 2, 1], weights)

    def apply(q):
        @pl.when(q + 1 < nsec)
        def _():
            mps_copy(q + 1).wait()
            psi_copy(q + 1).wait()

        pl.when(q + 2 < nsec)(lambda: right_copy(q + 2).wait())
        both = dot(as_left(beside(e_out[q])), as_right(states[q % 2], 0), 0)
        for state in (0, 1):
            value = both[:, state * width:(state + 1) * width] * coef[0, 0, 2 + state]
            value = dot(as_left(beside(value)), as_right(rights[(q + state) % 3], 1), 1)
            for i in range(in_sector):
                partial[q * in_sector + i, state] = value[i * unit:(i + 1) * unit]
        prepare_tensors(q + 1)
        prepare_right(q + 2)

        for i in range(in_sector):
            pair_copy(q * in_sector + i).start()

    def forward(q, chosen, first, arrived, copy):
        for i in range(in_sector):
            piece = q * in_sector + i
            owner_chip = piece // per // 2

            @pl.when(chosen(owner_chip))
            def _():
                pair_copy(piece).wait_recv()

                @pl.when(first)
                def _():
                    partial[piece, core] = partial[piece, core] + pair_in[piece]

                @pl.when(jnp.logical_not(first))
                def _():
                    copy(piece).wait_recv()
                    partial[piece, core] = (partial[piece, core] + pair_in[piece]) + arrived[piece]

                copy(piece).start()

    def upward(q):
        forward(q, lambda owner_chip: owner_chip > chip, chip == 0, up_in, up_copy)

    def downward(q):
        forward(q, lambda owner_chip: owner_chip < chip, chip == chips - 1, down_in, down_copy)

    def ending(q):
        for i in range(in_sector):
            piece = q * in_sector + i
            owner = piece // per

            @pl.when(owner // 2 == chip)
            def _():
                pair_copy(piece).wait_recv()
                partial[piece, core] = partial[piece, core] + pair_in[piece]

                @pl.when(chip > 0)
                def _():
                    up_copy(piece).wait_recv()
                    partial[piece, core] = partial[piece, core] + up_in[piece]

                @pl.when(chip < chips - 1)
                def _():
                    down_copy(piece).wait_recv()
                    partial[piece, core] = partial[piece, core] + down_in[piece]

                @pl.when(owner % 2 == core)
                def _():
                    target = pl.ds(pl.multiple_of((piece % per) * unit, unit), unit)
                    out[0, core, target, :] = partial[piece, core]

                pl.when(owner % 2 != core)(lambda: last_copy(piece).start())

    from_below, from_above = chip, chips - 1 - chip

    def turn(t, carry):
        @pl.when(t < nsec)
        def _():
            pl.when(leading & (t + LEAD < nsec))(lambda: tensor_copy(t + LEAD).start())
            update(t)
            apply(t)
            pl.when(odd & (t + 1 < nsec))(lambda: receive(t + 1))

        for stage, hops in (
            (upward, from_below),
            (downward, from_above),
            (ending, jnp.maximum(from_below, from_above)),
        ):
            q = t - FIRST_LAG - hops * HOP_LAG
            pl.when((q >= 0) & (q < nsec))(lambda: stage(q))
        return carry

    lax.fori_loop(0, nsec + FIRST_LAG + (chips - 1) * HOP_LAG, turn, 0)

    @pl.loop(0, nsec)
    def _(q):
        pl.when(odd)(lambda: swap_copy(q, core).wait_send())
        pl.when(odd & (site + 1 < sites))(lambda: e_copy(q).wait_send())
        pl.when(odd & (site + 2 < sites))(lambda: e_copy(q, 2).wait_send())
        pl.when(leading)(lambda: tensor_copy(q).wait_send())
        for i in range(in_sector):
            piece = q * in_sector + i
            owner_chip = piece // per // 2
            pair_copy(piece).wait_send()
            pl.when(owner_chip > chip)(lambda: up_copy(piece).wait_send())
            pl.when(owner_chip < chip)(lambda: down_copy(piece).wait_send())

    pl.when(leading)(lambda: coef_copy().wait_send())

    @pl.loop(0, per)
    def _(i):
        last_copy(i).wait()
        target = pl.ds(pl.multiple_of(i * unit, unit), unit)
        out[0, 1 - core, target, :] = last_in[i]


def shards(left_env, right_env, mps, psi, coef, sector_sizes, pattern):
    nsec, width = left_env.shape[1], left_env.shape[-1]
    sites, terms = lax.axis_size("site"), lax.axis_size("term")
    rows_owned = nsec * width // terms
    unit = math.gcd(rows_owned, width)
    pieces = nsec * width // unit
    per = rows_owned // unit
    block = (nsec, width, width)
    dma = pltpu.SemaphoreType.DMA
    hbm, smem = pl.BlockSpec(memory_space=pl.ANY), pl.BlockSpec(memory_space=pltpu.SMEM)
    return pl.pallas_call(
        functools.partial(kernel, sites, terms, unit),
        out_shape=jax.ShapeDtypeStruct((1, 2, rows_owned, width), jnp.float32),
        in_specs=[hbm] * 4 + [smem] * 3,
        out_specs=pl.BlockSpec(memory_space=pltpu.VMEM),
        scratch_shapes=[
            pltpu.VMEM(block, jnp.float32),
            pltpu.VMEM(block, jnp.float32),
            pltpu.VMEM(block, jnp.float32),
            pltpu.VMEM((2,) + block, jnp.float32),
            pltpu.VMEM((2,) + block, jnp.float32),
            pltpu.VMEM((pieces, 2, unit, width), jnp.float32),
            pltpu.VMEM((pieces, unit, width), jnp.float32),
            pltpu.VMEM((pieces, unit, width), jnp.float32),
            pltpu.VMEM((pieces, unit, width), jnp.float32),
            pltpu.VMEM((per, unit, width), jnp.float32),
            pltpu.VMEM((2, width, 2 * width), jnp.bfloat16),
            pltpu.VMEM((2, 2, width, 2 * width), jnp.bfloat16),
            pltpu.VMEM((2, 2 * width, 2 * width), jnp.bfloat16),
            pltpu.VMEM((3, width, 2 * width), jnp.bfloat16),
            pltpu.VMEM((2,) + block, jnp.float32),
            pltpu.VMEM((2, width, 2 * width), jnp.bfloat16),
            pltpu.VMEM((2, width, 2 * width), jnp.bfloat16),
            pltpu.VMEM((8, 128), jnp.float32),
            pltpu.VMEM((8, 128), jnp.float32),
            dma((nsec,)), dma((nsec,)), dma((nsec,)), dma((nsec,)),
            dma((nsec,)), dma((nsec,)),
            dma((pieces,)), dma((pieces,)), dma((pieces,)), dma((pieces,)), dma((pieces,)),
            dma((per,)), dma((per,)),
            dma((nsec,)), dma((nsec,)), dma((nsec,)), dma((nsec,)), dma((nsec,)), dma((2,)),
        ],
        compiler_params=pltpu.CompilerParams(
            collective_id=0, has_side_effects=True, vmem_limit_bytes=58 * 2**20
        ),
    )(left_env, right_env, mps, psi, coef, sector_sizes, pattern)


def solution(mesh):
    return jax.shard_map(
        shards,
        mesh=mesh,
        in_specs=(
            P("term", None, None, None),
            P("site", "term", None, None, None),
            P("site", None, None, None, None),
            P("site", None, None, None, None),
            P("site", "term", None),
            P(),
            P("term", None),
        ),
        out_specs=P("site", None, "term", None),
        check_vma=False,
    )
```

```python
import functools
import math

import jax
import jax.numpy as jnp
from jax import lax
from jax.experimental import pallas as pl
from jax.experimental.pallas import tpu as pltpu
from jax.sharding import PartitionSpec as P

MESH = pl.DeviceIdType.MESH
FIRST_LAG = 2
HOP_LAG = 1
LEAD = 4


def halves(x):
    high = x.astype(jnp.bfloat16)
    return high, (x - high.astype(jnp.float32)).astype(jnp.bfloat16)


def joined(parts, first, second, third, axis):
    width = parts.shape[axis] // 2
    pieces = [lax.slice_in_dim(parts, i * width, (i + 1) * width, axis=axis) for i in (0, 1)]
    return jnp.concatenate([pieces[first], pieces[second], pieces[third]], axis=axis)


def beside(x, axis=1):
    return jnp.concatenate(halves(x), axis=axis)


def dot(x, y, right_dim):
    return lax.dot_general(
        x, y, (((1,), (right_dim,)), ((), ())), preferred_element_type=jnp.float32
    )


def as_left(parts):
    return joined(parts, 0, 1, 0, 1)


def as_right(parts, axis):
    return joined(parts, 0, 0, 1, axis)


def kernel(
    sites, terms, unit,
    left, right, mps, psi, coef, sizes, pattern, out,
    e_in, e_out, right_v, mps_v, psi_v, partial, pair_in, up_in, down_in, last_in,
    tensors, states, rights,
    mps_in, shifted_v, earlier, coef_out, coef_in,
    left_sem, right_sem, mps_sem, psi_sem,
    e_send, e_recv, pair_send, pair_recv, z_send, up_recv, down_recv,
    last_send, last_recv,
    e_send_far, tensor_send, tensor_recv, swap_send, swap_recv, coef_sem,
):
    nsec, width = e_in.shape[0], e_in.shape[1]
    chips = terms // 2
    rows_owned = nsec * width // terms
    per = rows_owned // unit
    in_sector = width // unit
    site, term = lax.axis_index("site"), lax.axis_index("term")
    chip, core = term // 2, term % 2
    partner = chip * 2 + 1 - core
    odd = site % 2 == 1
    even = site % 2 == 0
    leading = even & (site < sites - 1)

    def left_copy(q):
        return pltpu.make_async_copy(left.at[0, q], e_in.at[q], left_sem.at[q])

    def right_copy(q):
        return pltpu.make_async_copy(right.at[0, 0, q], right_v.at[q], right_sem.at[q])

    def mps_copy(q):
        return pltpu.make_async_copy(mps.at[0, :, q], mps_v.at[:, q], mps_sem.at[q])

    def psi_copy(q):
        return pltpu.make_async_copy(psi.at[0, :, q], psi_v.at[:, q], psi_sem.at[q])

    @pl.loop(0, nsec)
    def _(q):
        pl.when(site < 2)(lambda: left_copy(q).start())

        mps_copy(q).start()
        psi_copy(q).start()
        right_copy(q).start()

    def e_copy(q, by=1):
        return pltpu.make_async_remote_copy(
            src_ref=e_out.at[q], dst_ref=e_in.at[q],
            send_sem=(e_send if by == 1 else e_send_far).at[q], recv_sem=e_recv.at[q],
            device_id={"site": jnp.minimum(site + by, sites - 1)}, device_id_type=MESH,
        )

    def tensor_copy(q):
        return pltpu.make_async_remote_copy(
            src_ref=mps.at[0, core, q], dst_ref=mps_in.at[core, q],
            send_sem=tensor_send.at[q], recv_sem=tensor_recv.at[q],
            device_id={"site": jnp.minimum(site + 1, sites - 1)}, device_id_type=MESH,
        )

    def swap_copy(q, state):
        return pltpu.make_async_remote_copy(
            src_ref=mps_in.at[state, q], dst_ref=mps_in.at[state, q],
            send_sem=swap_send.at[q], recv_sem=swap_recv.at[q],
            device_id={"term": partner}, device_id_type=MESH,
        )

    def coef_copy():
        return pltpu.make_async_remote_copy(
            src_ref=coef_out, dst_ref=coef_in,
            send_sem=coef_sem.at[0], recv_sem=coef_sem.at[1],
            device_id={"site": jnp.minimum(site + 1, sites - 1)}, device_id_type=MESH,
        )

    def pair_copy(piece):
        return pltpu.make_async_remote_copy(
            src_ref=partial.at[piece, 1 - core], dst_ref=pair_in.at[piece],
            send_sem=pair_send.at[piece], recv_sem=pair_recv.at[piece],
            device_id={"term": partner}, device_id_type=MESH,
        )

    def up_copy(piece):
        return pltpu.make_async_remote_copy(
            src_ref=partial.at[piece, core], dst_ref=up_in.at[piece],
            send_sem=z_send.at[piece], recv_sem=up_recv.at[piece],
            device_id={"term": jnp.minimum(term + 2, terms - 2 + core)}, device_id_type=MESH,
        )

    def down_copy(piece):
        return pltpu.make_async_remote_copy(
            src_ref=partial.at[piece, core], dst_ref=down_in.at[piece],
            send_sem=z_send.at[piece], recv_sem=down_recv.at[piece],
            device_id={"term": jnp.maximum(term - 2, core)}, device_id_type=MESH,
        )

    def last_copy(piece):
        return pltpu.make_async_remote_copy(
            src_ref=partial.at[piece, core], dst_ref=last_in.at[piece % per],
            send_sem=last_send.at[piece % per], recv_sem=last_recv.at[piece % per],
            device_id={"term": partner}, device_id_type=MESH,
        )

    barrier = pltpu.get_barrier_semaphore()
    greet = functools.partial(pl.semaphore_signal, barrier, inc=1, device_id_type=MESH)
    greet(device_id={"term": partner})
    pl.when(site > 0)(lambda: greet(device_id={"site": site - 1}))
    pl.when(site < sites - 1)(lambda: greet(device_id={"site": site + 1}))
    far_below, far_above = odd & (site > 1), odd & (site + 2 < sites)
    pl.when(far_below)(lambda: greet(device_id={"site": site - 2}))
    pl.when(far_above)(lambda: greet(device_id={"site": site + 2}))
    pl.when(chip > 0)(lambda: greet(device_id={"term": term - 2}))
    pl.when(chip < chips - 1)(lambda: greet(device_id={"term": term + 2}))
    bounds = (site > 0, site < sites - 1, far_below, far_above, chip > 0, chip < chips - 1)
    peers = 1
    for met in bounds:
        peers = peers + jnp.where(met, 1, 0)
    pl.semaphore_wait(barrier, peers)

    lanes = lax.broadcasted_iota(jnp.int32, coef_out.shape, 1)
    coef_out[...] = jnp.where(lanes == 0, coef[0, 0, 0], coef[0, 0, 1])

    @pl.when(leading)
    def _():
        coef_copy().start()
        pl.loop(0, min(LEAD, nsec))(lambda q: tensor_copy(q).start())

    rows = lax.broadcasted_iota(jnp.int32, (width, width), 0)
    columns = lax.broadcasted_iota(jnp.int32, (width, width), 1)

    def framed(x, high, wide):
        return jnp.where((rows < high) & (columns < wide), x, 0.0)

    def prepare_right(h):
        held = jnp.minimum(h, nsec - 1)
        size = jnp.where(h < nsec, sizes[held], 0)
        there = pattern[0, held].astype(jnp.float32)
        rights[h % 3] = beside(framed(right_v[held], size, size) * there)

    def pair_of(blocks, same_q, size, size_after):
        same = beside(framed(blocks[0, same_q], size, size).T)
        step = beside(framed(blocks[1, same_q], size, size_after).T)
        return same, step

    def sizes_at(q):
        return sizes[q], jnp.where(q + 1 < nsec, sizes[jnp.minimum(q + 1, nsec - 1)], 0)

    def prepare_tensors(h):
        q = jnp.minimum(h, nsec - 1)
        tensors[h % 2, 0], tensors[h % 2, 1] = pair_of(mps_v, q, *sizes_at(q))

    def prepare_states(q):
        size, size_after = sizes_at(q)
        states[q % 2] = jnp.concatenate(
            [
                beside(framed(psi_v[0, q], size, size), 0),
                beside(framed(psi_v[1, q], size, size_after), 0),
            ],
            axis=1,
        )

    tensors[1] = jnp.zeros(tensors.shape[1:], jnp.bfloat16)
    earlier[1] = jnp.zeros(tensors.shape[1:], jnp.bfloat16)
    shifted_v[...] = jnp.zeros(shifted_v.shape, jnp.bfloat16)
    e_out[0] = jnp.zeros((width, width), jnp.float32)
    states[0] = jnp.zeros((2 * width, 2 * width), jnp.bfloat16)
    rights[1] = jnp.zeros((width, 2 * width), jnp.bfloat16)
    mps_copy(0).wait()
    right_copy(0).wait()
    prepare_tensors(0)
    prepare_right(0)

    def receive(q):
        tensor_copy(q).wait_recv()
        swap_copy(q, core).start()

    @pl.when(odd)
    def _():
        coef_copy().wait_recv()
        receive(0)

    def advanced(block, q, held, kept, weights):
        joint = jnp.concatenate([as_right(held[q % 2, 0], 1), as_right(held[q % 2, 1], 1)], axis=0)
        both = dot(as_left(beside(block)), joint, 1)
        here = beside(both[:, :width] * weights[0], 0)
        same = dot(as_left(held[q % 2, 0]), as_right(here, 0), 0)
        step = dot(as_left(held[(q + 1) % 2, 1]), as_right(kept[...], 0), 0)
        kept[...] = beside(both[:, width:] * weights[1], 0)
        return same + step

    def applied(q):
        environ = as_left(beside(e_out[q]))
        both = dot(environ, as_right(states[(q + 2) % 2], 0), 0)
        for state in (0, 1):
            value = both[:, state * width:(state + 1) * width] * coef[0, 0, 2 + state]
            value = dot(as_left(beside(value)), as_right(rights[(q + state) % 3], 1), 1)
            for i in range(in_sector):
                partial[q * in_sector + i, state] = value[i * unit:(i + 1) * unit]

    def send_pair(q):
        for i in range(in_sector):
            pair_copy(q * in_sector + i).start()

    def work(t):
        before, after = jnp.maximum(t - 1, 0), jnp.minimum(t + 1, nsec - 1)
        psi_copy(t).wait()

        @pl.when(t + 1 < nsec)
        def _():
            mps_copy(t + 1).wait()
            right_copy(t + 1).wait()

        pl.when(site < 2)(lambda: left_copy(t).wait())
        pl.when(odd)(lambda: swap_copy(t, 1 - core).wait_recv())
        pl.when(site > 1)(lambda: e_copy(t).wait_recv())
        size = sizes[t]
        first = jnp.where(site < 2, pattern[0, t].astype(jnp.float32), 1.0)
        weights = coef[0, 0, 0], coef[0, 0, 1]

        @pl.when(odd)
        def _():
            earlier[t % 2, 0], earlier[t % 2, 1] = pair_of(mps_in, t, *sizes_at(t))
            block = framed(e_in[t], size, size) * first
            weights_in = coef_in[0:1, 0:1], coef_in[0:1, 1:2]
            middle = advanced(block, t, earlier, shifted_v.at[1], weights_in)
            applied(before)
            e_out[t] = advanced(middle, t, tensors, shifted_v.at[0], weights)
            prepare_tensors(t + 1)
            prepare_states(t)
            prepare_right(t + 1)

        pl.when(odd & (site + 1 < sites))(lambda: e_copy(t).start())
        pl.when(odd & (site + 2 < sites))(lambda: e_copy(t, 2).start())

        @pl.when(even)
        def _():
            block = framed(e_in[t], size, size) * first
            applied(before)
            e_out[t] = advanced(block, t, tensors, shifted_v.at[0], weights)
            prepare_tensors(t + 1)
            prepare_states(t)
            prepare_right(t + 1)

        pl.when(t > 0)(lambda: send_pair(before))

    def forward(q, chosen, first, arrived, copy):
        for i in range(in_sector):
            piece = q * in_sector + i
            owner_chip = piece // per // 2

            @pl.when(chosen(owner_chip))
            def _():
                pair_copy(piece).wait_recv()

                @pl.when(first)
                def _():
                    partial[piece, core] = partial[piece, core] + pair_in[piece]

                @pl.when(jnp.logical_not(first))
                def _():
                    copy(piece).wait_recv()
                    partial[piece, core] = (partial[piece, core] + pair_in[piece]) + arrived[piece]

                copy(piece).start()

    def upward(q):
        forward(q, lambda owner_chip: owner_chip > chip, chip == 0, up_in, up_copy)

    def downward(q):
        forward(q, lambda owner_chip: owner_chip < chip, chip == chips - 1, down_in, down_copy)

    def ending(q):
        for i in range(in_sector):
            piece = q * in_sector + i
            owner = piece // per

            @pl.when(owner // 2 == chip)
            def _():
                pair_copy(piece).wait_recv()
                partial[piece, core] = partial[piece, core] + pair_in[piece]

                @pl.when(chip > 0)
                def _():
                    up_copy(piece).wait_recv()
                    partial[piece, core] = partial[piece, core] + up_in[piece]

                @pl.when(chip < chips - 1)
                def _():
                    down_copy(piece).wait_recv()
                    partial[piece, core] = partial[piece, core] + down_in[piece]

                @pl.when(owner % 2 == core)
                def _():
                    target = pl.ds(pl.multiple_of((piece % per) * unit, unit), unit)
                    out[0, core, target, :] = partial[piece, core]

                pl.when(owner % 2 != core)(lambda: last_copy(piece).start())

    from_below, from_above = chip, chips - 1 - chip

    def turn(t, carry):
        @pl.when(t < nsec)
        def _():
            pl.when(leading & (t + LEAD < nsec))(lambda: tensor_copy(t + LEAD).start())
            work(t)
            pl.when(odd & (t + 1 < nsec))(lambda: receive(t + 1))

        @pl.when(t == nsec)
        def _():
            applied(nsec - 1)
            send_pair(nsec - 1)

        for stage, hops in (
            (upward, from_below),
            (downward, from_above),
            (ending, jnp.maximum(from_below, from_above)),
        ):
            q = t - FIRST_LAG - hops * HOP_LAG
            pl.when((q >= 0) & (q < nsec))(lambda: stage(q))
        return carry

    lax.fori_loop(0, nsec + FIRST_LAG + (chips - 1) * HOP_LAG, turn, 0)

    @pl.loop(0, nsec)
    def _(q):
        pl.when(odd)(lambda: swap_copy(q, core).wait_send())
        pl.when(odd & (site + 1 < sites))(lambda: e_copy(q).wait_send())
        pl.when(odd & (site + 2 < sites))(lambda: e_copy(q, 2).wait_send())
        pl.when(leading)(lambda: tensor_copy(q).wait_send())
        for i in range(in_sector):
            piece = q * in_sector + i
            owner_chip = piece // per // 2
            pair_copy(piece).wait_send()
            pl.when(owner_chip > chip)(lambda: up_copy(piece).wait_send())
            pl.when(owner_chip < chip)(lambda: down_copy(piece).wait_send())

    pl.when(leading)(lambda: coef_copy().wait_send())

    @pl.loop(0, per)
    def _(i):
        last_copy(i).wait()
        target = pl.ds(pl.multiple_of(i * unit, unit), unit)
        out[0, 1 - core, target, :] = last_in[i]


def shards(left_env, right_env, mps, psi, coef, sector_sizes, pattern):
    nsec, width = left_env.shape[1], left_env.shape[-1]
    sites, terms = lax.axis_size("site"), lax.axis_size("term")
    rows_owned = nsec * width // terms
    unit = math.gcd(rows_owned, width)
    pieces = nsec * width // unit
    per = rows_owned // unit
    block = (nsec, width, width)
    dma = pltpu.SemaphoreType.DMA
    hbm, smem = pl.BlockSpec(memory_space=pl.ANY), pl.BlockSpec(memory_space=pltpu.SMEM)
    return pl.pallas_call(
        functools.partial(kernel, sites, terms, unit),
        out_shape=jax.ShapeDtypeStruct((1, 2, rows_owned, width), jnp.float32),
        in_specs=[hbm] * 4 + [smem] * 3,
        out_specs=pl.BlockSpec(memory_space=pltpu.VMEM),
        scratch_shapes=[
            pltpu.VMEM(block, jnp.float32),
            pltpu.VMEM(block, jnp.float32),
            pltpu.VMEM(block, jnp.float32),
            pltpu.VMEM((2,) + block, jnp.float32),
            pltpu.VMEM((2,) + block, jnp.float32),
            pltpu.VMEM((pieces, 2, unit, width), jnp.float32),
            pltpu.VMEM((pieces, unit, width), jnp.float32),
            pltpu.VMEM((pieces, unit, width), jnp.float32),
            pltpu.VMEM((pieces, unit, width), jnp.float32),
            pltpu.VMEM((per, unit, width), jnp.float32),
            pltpu.VMEM((2, 2, width, 2 * width), jnp.bfloat16),
            pltpu.VMEM((2, 2 * width, 2 * width), jnp.bfloat16),
            pltpu.VMEM((3, width, 2 * width), jnp.bfloat16),
            pltpu.VMEM((2,) + block, jnp.float32),
            pltpu.VMEM((2, 2 * width, width), jnp.bfloat16),
            pltpu.VMEM((2, 2, width, 2 * width), jnp.bfloat16),
            pltpu.VMEM((8, 128), jnp.float32),
            pltpu.VMEM((8, 128), jnp.float32),
            dma((nsec,)), dma((nsec,)), dma((nsec,)), dma((nsec,)),
            dma((nsec,)), dma((nsec,)),
            dma((pieces,)), dma((pieces,)), dma((pieces,)), dma((pieces,)), dma((pieces,)),
            dma((per,)), dma((per,)),
            dma((nsec,)), dma((nsec,)), dma((nsec,)), dma((nsec,)), dma((nsec,)), dma((2,)),
        ],
        compiler_params=pltpu.CompilerParams(
            collective_id=0, has_side_effects=True, vmem_limit_bytes=58 * 2**20
        ),
    )(left_env, right_env, mps, psi, coef, sector_sizes, pattern)


def solution(mesh):
    return jax.shard_map(
        shards,
        mesh=mesh,
        in_specs=(
            P("term", None, None, None),
            P("site", "term", None, None, None),
            P("site", None, None, None, None),
            P("site", None, None, None, None),
            P("site", "term", None),
            P(),
            P("term", None),
        ),
        out_specs=P("site", None, "term", None),
        check_vma=False,
    )
```

```python
import functools
import math

import jax
import jax.numpy as jnp
from jax import lax
from jax.experimental import pallas as pl
from jax.experimental.pallas import tpu as pltpu
from jax.sharding import PartitionSpec as P

MESH = pl.DeviceIdType.MESH
FIRST_LAG = 1
HOP_LAG = 1
LEAD = 4


def halves(x):
    high = x.astype(jnp.bfloat16)
    return high, (x - high.astype(jnp.float32)).astype(jnp.bfloat16)


def joined(parts, first, second, third, axis):
    width = parts.shape[axis] // 2
    pieces = [lax.slice_in_dim(parts, i * width, (i + 1) * width, axis=axis) for i in (0, 1)]
    return jnp.concatenate([pieces[first], pieces[second], pieces[third]], axis=axis)


def beside(x, axis=1):
    return jnp.concatenate(halves(x), axis=axis)


def dot(x, y, right_dim):
    return lax.dot_general(
        x, y, (((1,), (right_dim,)), ((), ())), preferred_element_type=jnp.float32
    )


def as_left(parts):
    return joined(parts, 0, 1, 0, 1)


def as_right(parts, axis):
    return joined(parts, 0, 0, 1, axis)


def kernel(
    sites, terms, unit,
    left, right, mps, psi, coef, sizes, pattern, out,
    e_in, e_out, right_v, mps_v, psi_v, partial, pair_in, up_in, down_in, last_in,
    environs, tensors, states, rights,
    mps_in, middles, earlier, coef_out, coef_in,
    left_sem, right_sem, mps_sem, psi_sem,
    e_send, e_recv, pair_send, pair_recv, z_send, up_recv, down_recv,
    last_send, last_recv,
    e_send_far, tensor_send, tensor_recv, swap_send, swap_recv, coef_sem,
):
    nsec, width = e_in.shape[0], e_in.shape[1]
    chips = terms // 2
    rows_owned = nsec * width // terms
    per = rows_owned // unit
    in_sector = width // unit
    site, term = lax.axis_index("site"), lax.axis_index("term")
    chip, core = term // 2, term % 2
    partner = chip * 2 + 1 - core
    odd = site % 2 == 1
    even = site % 2 == 0
    leading = even & (site < sites - 1)

    def left_copy(q):
        return pltpu.make_async_copy(left.at[0, q], e_in.at[q], left_sem.at[q])

    def right_copy(q):
        return pltpu.make_async_copy(right.at[0, 0, q], right_v.at[q], right_sem.at[q])

    def mps_copy(q):
        return pltpu.make_async_copy(mps.at[0, :, q], mps_v.at[:, q], mps_sem.at[q])

    def psi_copy(q):
        return pltpu.make_async_copy(psi.at[0, :, q], psi_v.at[:, q], psi_sem.at[q])

    @pl.loop(0, nsec)
    def _(q):
        pl.when(site < 2)(lambda: left_copy(q).start())

        mps_copy(q).start()
        psi_copy(q).start()
        right_copy(q).start()

    def e_copy(q, by=1):
        return pltpu.make_async_remote_copy(
            src_ref=e_out.at[q], dst_ref=e_in.at[q],
            send_sem=(e_send if by == 1 else e_send_far).at[q], recv_sem=e_recv.at[q],
            device_id={"site": jnp.minimum(site + by, sites - 1)}, device_id_type=MESH,
        )

    def tensor_copy(q):
        return pltpu.make_async_remote_copy(
            src_ref=mps.at[0, core, q], dst_ref=mps_in.at[core, q],
            send_sem=tensor_send.at[q], recv_sem=tensor_recv.at[q],
            device_id={"site": jnp.minimum(site + 1, sites - 1)}, device_id_type=MESH,
        )

    def swap_copy(q, state):
        return pltpu.make_async_remote_copy(
            src_ref=mps_in.at[state, q], dst_ref=mps_in.at[state, q],
            send_sem=swap_send.at[q], recv_sem=swap_recv.at[q],
            device_id={"term": partner}, device_id_type=MESH,
        )

    def coef_copy():
        return pltpu.make_async_remote_copy(
            src_ref=coef_out, dst_ref=coef_in,
            send_sem=coef_sem.at[0], recv_sem=coef_sem.at[1],
            device_id={"site": jnp.minimum(site + 1, sites - 1)}, device_id_type=MESH,
        )

    def pair_copy(piece):
        return pltpu.make_async_remote_copy(
            src_ref=partial.at[piece, 1 - core], dst_ref=pair_in.at[piece],
            send_sem=pair_send.at[piece], recv_sem=pair_recv.at[piece],
            device_id={"term": partner}, device_id_type=MESH,
        )

    def up_copy(piece):
        return pltpu.make_async_remote_copy(
            src_ref=partial.at[piece, core], dst_ref=up_in.at[piece],
            send_sem=z_send.at[piece], recv_sem=up_recv.at[piece],
            device_id={"term": jnp.minimum(term + 2, terms - 2 + core)}, device_id_type=MESH,
        )

    def down_copy(piece):
        return pltpu.make_async_remote_copy(
            src_ref=partial.at[piece, core], dst_ref=down_in.at[piece],
            send_sem=z_send.at[piece], recv_sem=down_recv.at[piece],
            device_id={"term": jnp.maximum(term - 2, core)}, device_id_type=MESH,
        )

    def last_copy(piece):
        return pltpu.make_async_remote_copy(
            src_ref=partial.at[piece, core], dst_ref=last_in.at[piece % per],
            send_sem=last_send.at[piece % per], recv_sem=last_recv.at[piece % per],
            device_id={"term": partner}, device_id_type=MESH,
        )

    barrier = pltpu.get_barrier_semaphore()
    greet = functools.partial(pl.semaphore_signal, barrier, inc=1, device_id_type=MESH)
    greet(device_id={"term": partner})
    pl.when(site > 0)(lambda: greet(device_id={"site": site - 1}))
    pl.when(site < sites - 1)(lambda: greet(device_id={"site": site + 1}))
    far_below, far_above = odd & (site > 1), odd & (site + 2 < sites)
    pl.when(far_below)(lambda: greet(device_id={"site": site - 2}))
    pl.when(far_above)(lambda: greet(device_id={"site": site + 2}))
    pl.when(chip > 0)(lambda: greet(device_id={"term": term - 2}))
    pl.when(chip < chips - 1)(lambda: greet(device_id={"term": term + 2}))
    bounds = (site > 0, site < sites - 1, far_below, far_above, chip > 0, chip < chips - 1)
    peers = 1
    for met in bounds:
        peers = peers + jnp.where(met, 1, 0)
    pl.semaphore_wait(barrier, peers)

    lanes = lax.broadcasted_iota(jnp.int32, coef_out.shape, 1)
    coef_out[...] = jnp.where(lanes == 0, coef[0, 0, 0], coef[0, 0, 1])

    @pl.when(leading)
    def _():
        coef_copy().start()
        pl.loop(0, min(LEAD, nsec))(lambda q: tensor_copy(q).start())

    rows = lax.broadcasted_iota(jnp.int32, (width, width), 0)
    columns = lax.broadcasted_iota(jnp.int32, (width, width), 1)

    def framed(x, high, wide):
        return jnp.where((rows < high) & (columns < wide), x, 0.0)

    def prepare_right(h):
        held = jnp.minimum(h, nsec - 1)
        size = jnp.where(h < nsec, sizes[held], 0)
        there = pattern[0, held].astype(jnp.float32)
        rights[h % 3] = beside(framed(right_v[held], size, size) * there)

    def prepare_tensors(h):
        q = jnp.minimum(h, nsec - 1)
        before, after = jnp.maximum(q - 1, 0), jnp.minimum(q + 1, nsec - 1)
        size, size_before = sizes[q], sizes[before]
        size_after = jnp.where(q + 1 < nsec, sizes[after], 0)
        tensors[h % 2, 0] = beside(framed(mps_v[0, q], size, size).T)
        tensors[h % 2, 1] = beside(framed(mps_v[1, before], size_before, size).T)
        states[h % 2] = jnp.concatenate(
            [
                beside(framed(psi_v[0, q], size, size), 0),
                beside(framed(psi_v[1, q], size, size_after), 0),
            ],
            axis=1,
        )

    environs[1] = jnp.zeros((width, 2 * width), jnp.bfloat16)
    middles[1] = jnp.zeros((width, 2 * width), jnp.bfloat16)
    mps_copy(0).wait()
    psi_copy(0).wait()
    right_copy(0).wait()
    right_copy(1).wait()
    prepare_tensors(0)
    prepare_right(0)
    prepare_right(1)

    def receive(q):
        tensor_copy(q).wait_recv()
        swap_copy(q, core).start()

    @pl.when(odd)
    def _():
        coef_copy().wait_recv()
        receive(0)

    def advanced(blocks, q, same, step, weights):
        here = dot(as_left(blocks[q % 2]), as_right(same, 1), 1) * weights[0]
        shifted = dot(as_left(blocks[(q + 1) % 2]), as_right(step, 1), 1) * weights[1]
        return dot(
            jnp.concatenate([as_left(same), as_left(step)], axis=1),
            jnp.concatenate([as_right(beside(here, 0), 0), as_right(beside(shifted, 0), 0)], axis=0),
            0,
        )

    def update(q):
        before = jnp.maximum(q - 1, 0)
        pl.when(site < 2)(lambda: left_copy(q).wait())
        pl.when(site > 1)(lambda: e_copy(q).wait_recv())
        size, size_before = sizes[q], sizes[before]
        first = jnp.where(site < 2, pattern[0, q].astype(jnp.float32), 1.0)
        below = jnp.where(q > 0, 1.0, 0.0)
        weights = coef[0, 0, 0], coef[0, 0, 1] * below

        @pl.when(odd)
        def _():
            swap_copy(q, 1 - core).wait_recv()
            earlier[0] = beside(framed(mps_in[0, q], size, size).T)
            earlier[1] = beside(framed(mps_in[1, before], size_before, size).T)
            environs[q % 2] = beside(framed(e_in[q], size, size) * first)
            weights_in = coef_in[0:1, 0:1], coef_in[0:1, 1:2] * below
            middle = advanced(environs, q, earlier[0], earlier[1], weights_in)
            middles[q % 2] = beside(middle)
            e_out[q] = advanced(middles, q, tensors[q % 2, 0], tensors[q % 2, 1], weights)
            pl.when(site + 1 < sites)(lambda: e_copy(q).start())
            pl.when(site + 2 < sites)(lambda: e_copy(q, 2).start())

        @pl.when(even)
        def _():
            environs[q % 2] = beside(framed(e_in[q], size, size) * first)
            e_out[q] = advanced(environs, q, tensors[q % 2, 0], tensors[q % 2, 1], weights)

    def apply(q):
        @pl.when(q + 1 < nsec)
        def _():
            mps_copy(q + 1).wait()
            psi_copy(q + 1).wait()

        pl.when(q + 2 < nsec)(lambda: right_copy(q + 2).wait())
        both = dot(as_left(beside(e_out[q])), as_right(states[q % 2], 0), 0)
        for state in (0, 1):
            value = both[:, state * width:(state + 1) * width] * coef[0, 0, 2 + state]
            value = dot(as_left(beside(value)), as_right(rights[(q + state) % 3], 1), 1)
            for i in range(in_sector):
                partial[q * in_sector + i, state] = value[i * unit:(i + 1) * unit]
        prepare_tensors(q + 1)
        prepare_right(q + 2)

        for i in range(in_sector):
            pair_copy(q * in_sector + i).start()

    def forward(q, chosen, first, arrived, copy):
        for i in range(in_sector):
            piece = q * in_sector + i
            owner_chip = piece // per // 2

            @pl.when(chosen(owner_chip))
            def _():
                pair_copy(piece).wait_recv()

                @pl.when(first)
                def _():
                    partial[piece, core] = partial[piece, core] + pair_in[piece]

                @pl.when(jnp.logical_not(first))
                def _():
                    copy(piece).wait_recv()
                    partial[piece, core] = (partial[piece, core] + pair_in[piece]) + arrived[piece]

                copy(piece).start()

    def upward(q):
        forward(q, lambda owner_chip: owner_chip > chip, chip == 0, up_in, up_copy)

    def downward(q):
        forward(q, lambda owner_chip: owner_chip < chip, chip == chips - 1, down_in, down_copy)

    def ending(q):
        for i in range(in_sector):
            piece = q * in_sector + i
            owner = piece // per

            @pl.when(owner // 2 == chip)
            def _():
                pair_copy(piece).wait_recv()
                partial[piece, core] = partial[piece, core] + pair_in[piece]

                @pl.when(chip > 0)
                def _():
                    up_copy(piece).wait_recv()
                    partial[piece, core] = partial[piece, core] + up_in[piece]

                @pl.when(chip < chips - 1)
                def _():
                    down_copy(piece).wait_recv()
                    partial[piece, core] = partial[piece, core] + down_in[piece]

                @pl.when(owner % 2 == core)
                def _():
                    target = pl.ds(pl.multiple_of((piece % per) * unit, unit), unit)
                    out[0, core, target, :] = partial[piece, core]

                pl.when(owner % 2 != core)(lambda: last_copy(piece).start())

    from_below, from_above = chip, chips - 1 - chip

    last = site + 2 >= sites

    def reduction(t):
        for stage, hops in (
            (upward, from_below),
            (downward, from_above),
            (ending, jnp.maximum(from_below, from_above)),
        ):
            q = t - FIRST_LAG - hops * HOP_LAG
            pl.when((q >= 0) & (q < nsec))(lambda: stage(q))

    def turn(t, carry):
        pl.when(last)(lambda: reduction(t))

        @pl.when(t < nsec)
        def _():
            pl.when(leading & (t + LEAD < nsec))(lambda: tensor_copy(t + LEAD).start())
            update(t)
            apply(t)
            pl.when(odd & (t + 1 < nsec))(lambda: receive(t + 1))

        pl.when(jnp.logical_not(last))(lambda: reduction(t))
        return carry

    lax.fori_loop(0, nsec + FIRST_LAG + (chips - 1) * HOP_LAG, turn, 0)

    @pl.loop(0, nsec)
    def _(q):
        pl.when(odd)(lambda: swap_copy(q, core).wait_send())
        pl.when(odd & (site + 1 < sites))(lambda: e_copy(q).wait_send())
        pl.when(odd & (site + 2 < sites))(lambda: e_copy(q, 2).wait_send())
        pl.when(leading)(lambda: tensor_copy(q).wait_send())
        for i in range(in_sector):
            piece = q * in_sector + i
            owner_chip = piece // per // 2
            pair_copy(piece).wait_send()
            pl.when(owner_chip > chip)(lambda: up_copy(piece).wait_send())
            pl.when(owner_chip < chip)(lambda: down_copy(piece).wait_send())

    pl.when(leading)(lambda: coef_copy().wait_send())

    @pl.loop(0, per)
    def _(i):
        last_copy(i).wait()
        target = pl.ds(pl.multiple_of(i * unit, unit), unit)
        out[0, 1 - core, target, :] = last_in[i]


def shards(left_env, right_env, mps, psi, coef, sector_sizes, pattern):
    nsec, width = left_env.shape[1], left_env.shape[-1]
    sites, terms = lax.axis_size("site"), lax.axis_size("term")
    rows_owned = nsec * width // terms
    unit = math.gcd(rows_owned, width)
    pieces = nsec * width // unit
    per = rows_owned // unit
    block = (nsec, width, width)
    dma = pltpu.SemaphoreType.DMA
    hbm, smem = pl.BlockSpec(memory_space=pl.ANY), pl.BlockSpec(memory_space=pltpu.SMEM)
    return pl.pallas_call(
        functools.partial(kernel, sites, terms, unit),
        out_shape=jax.ShapeDtypeStruct((1, 2, rows_owned, width), jnp.float32),
        in_specs=[hbm] * 4 + [smem] * 3,
        out_specs=pl.BlockSpec(memory_space=pltpu.VMEM),
        scratch_shapes=[
            pltpu.VMEM(block, jnp.float32),
            pltpu.VMEM(block, jnp.float32),
            pltpu.VMEM(block, jnp.float32),
            pltpu.VMEM((2,) + block, jnp.float32),
            pltpu.VMEM((2,) + block, jnp.float32),
            pltpu.VMEM((pieces, 2, unit, width), jnp.float32),
            pltpu.VMEM((pieces, unit, width), jnp.float32),
            pltpu.VMEM((pieces, unit, width), jnp.float32),
            pltpu.VMEM((pieces, unit, width), jnp.float32),
            pltpu.VMEM((per, unit, width), jnp.float32),
            pltpu.VMEM((2, width, 2 * width), jnp.bfloat16),
            pltpu.VMEM((2, 2, width, 2 * width), jnp.bfloat16),
            pltpu.VMEM((2, 2 * width, 2 * width), jnp.bfloat16),
            pltpu.VMEM((3, width, 2 * width), jnp.bfloat16),
            pltpu.VMEM((2,) + block, jnp.float32),
            pltpu.VMEM((2, width, 2 * width), jnp.bfloat16),
            pltpu.VMEM((2, width, 2 * width), jnp.bfloat16),
            pltpu.VMEM((8, 128), jnp.float32),
            pltpu.VMEM((8, 128), jnp.float32),
            dma((nsec,)), dma((nsec,)), dma((nsec,)), dma((nsec,)),
            dma((nsec,)), dma((nsec,)),
            dma((pieces,)), dma((pieces,)), dma((pieces,)), dma((pieces,)), dma((pieces,)),
            dma((per,)), dma((per,)),
            dma((nsec,)), dma((nsec,)), dma((nsec,)), dma((nsec,)), dma((nsec,)), dma((2,)),
        ],
        compiler_params=pltpu.CompilerParams(
            collective_id=0, has_side_effects=True, vmem_limit_bytes=58 * 2**20
        ),
    )(left_env, right_env, mps, psi, coef, sector_sizes, pattern)


def solution(mesh):
    return jax.shard_map(
        shards,
        mesh=mesh,
        in_specs=(
            P("term", None, None, None),
            P("site", "term", None, None, None),
            P("site", None, None, None, None),
            P("site", None, None, None, None),
            P("site", "term", None),
            P(),
            P("term", None),
        ),
        out_specs=P("site", None, "term", None),
        check_vma=False,
    )
```

```python
import functools
import math

import jax
import jax.numpy as jnp
from jax import lax
from jax.experimental import pallas as pl
from jax.experimental.pallas import tpu as pltpu
from jax.sharding import PartitionSpec as P

MESH = pl.DeviceIdType.MESH
FIRST_LAG = 1
HOP_LAG = 1
LEAD = 4


def halves(x):
    high = x.astype(jnp.bfloat16)
    return high, (x - high.astype(jnp.float32)).astype(jnp.bfloat16)


def joined(parts, first, second, third, axis):
    width = parts.shape[axis] // 2
    pieces = [lax.slice_in_dim(parts, i * width, (i + 1) * width, axis=axis) for i in (0, 1)]
    return jnp.concatenate([pieces[first], pieces[second], pieces[third]], axis=axis)


def beside(x, axis=1):
    return jnp.concatenate(halves(x), axis=axis)


def dot(x, y, right_dim):
    return lax.dot_general(
        x, y, (((1,), (right_dim,)), ((), ())), preferred_element_type=jnp.float32
    )


def as_left(parts):
    return joined(parts, 0, 1, 0, 1)


def as_right(parts, axis):
    return joined(parts, 0, 0, 1, axis)


def kernel(
    sites, terms, unit,
    left, right, mps, psi, coef, sizes, pattern, out,
    e_in, e_out, right_v, mps_v, psi_v, partial, pair_in, up_in, down_in, last_in,
    environs, tensors, states, rights,
    mps_in, middles, earlier, coef_out, coef_in,
    left_sem, right_sem, mps_sem, psi_sem,
    e_send, e_recv, pair_send, pair_recv, z_send, up_recv, down_recv,
    last_send, last_recv,
    e_send_far, tensor_send, tensor_recv, swap_send, swap_recv, coef_sem,
):
    nsec, width = e_in.shape[0], e_in.shape[1]
    chips = terms // 2
    rows_owned = nsec * width // terms
    per = rows_owned // unit
    in_sector = width // unit
    site, term = lax.axis_index("site"), lax.axis_index("term")
    chip, core = term // 2, term % 2
    partner = chip * 2 + 1 - core
    odd = site % 2 == 1
    even = site % 2 == 0
    leading = even & (site < sites - 1)

    def left_copy(q):
        return pltpu.make_async_copy(left.at[0, q], e_in.at[q], left_sem.at[q])

    def right_copy(q):
        return pltpu.make_async_copy(right.at[0, 0, q], right_v.at[q], right_sem.at[q])

    def mps_copy(q):
        return pltpu.make_async_copy(mps.at[0, :, q], mps_v.at[:, q], mps_sem.at[q])

    def psi_copy(q):
        return pltpu.make_async_copy(psi.at[0, :, q], psi_v.at[:, q], psi_sem.at[q])

    @pl.loop(0, nsec)
    def _(q):
        pl.when(site < 2)(lambda: left_copy(q).start())

        mps_copy(q).start()
        psi_copy(q).start()
        right_copy(q).start()

    def e_copy(q, by=1):
        return pltpu.make_async_remote_copy(
            src_ref=e_out.at[q], dst_ref=e_in.at[q],
            send_sem=(e_send if by == 1 else e_send_far).at[q], recv_sem=e_recv.at[q],
            device_id={"site": jnp.minimum(site + by, sites - 1)}, device_id_type=MESH,
        )

    def tensor_copy(q):
        return pltpu.make_async_remote_copy(
            src_ref=mps.at[0, core, q], dst_ref=mps_in.at[core, q],
            send_sem=tensor_send.at[q], recv_sem=tensor_recv.at[q],
            device_id={"site": jnp.minimum(site + 1, sites - 1)}, device_id_type=MESH,
        )

    def needed(q, state):
        return (state == 0) | (q < nsec - 1)

    def swap_copy(q, state):
        return pltpu.make_async_remote_copy(
            src_ref=mps_in.at[state, q], dst_ref=mps_in.at[state, q],
            send_sem=swap_send.at[q], recv_sem=swap_recv.at[q],
            device_id={"term": partner}, device_id_type=MESH,
        )

    def coef_copy():
        return pltpu.make_async_remote_copy(
            src_ref=coef_out, dst_ref=coef_in,
            send_sem=coef_sem.at[0], recv_sem=coef_sem.at[1],
            device_id={"site": jnp.minimum(site + 1, sites - 1)}, device_id_type=MESH,
        )

    def pair_copy(piece):
        return pltpu.make_async_remote_copy(
            src_ref=partial.at[piece, 1 - core], dst_ref=pair_in.at[piece],
            send_sem=pair_send.at[piece], recv_sem=pair_recv.at[piece],
            device_id={"term": partner}, device_id_type=MESH,
        )

    def up_copy(piece):
        return pltpu.make_async_remote_copy(
            src_ref=partial.at[piece, core], dst_ref=up_in.at[piece],
            send_sem=z_send.at[piece], recv_sem=up_recv.at[piece],
            device_id={"term": jnp.minimum(term + 2, terms - 2 + core)}, device_id_type=MESH,
        )

    def down_copy(piece):
        return pltpu.make_async_remote_copy(
            src_ref=partial.at[piece, core], dst_ref=down_in.at[piece],
            send_sem=z_send.at[piece], recv_sem=down_recv.at[piece],
            device_id={"term": jnp.maximum(term - 2, core)}, device_id_type=MESH,
        )

    def last_copy(piece):
        return pltpu.make_async_remote_copy(
            src_ref=partial.at[piece, core], dst_ref=last_in.at[piece % per],
            send_sem=last_send.at[piece % per], recv_sem=last_recv.at[piece % per],
            device_id={"term": partner}, device_id_type=MESH,
        )

    barrier = pltpu.get_barrier_semaphore()
    greet = functools.partial(pl.semaphore_signal, barrier, inc=1, device_id_type=MESH)
    greet(device_id={"term": partner})
    pl.when(site > 0)(lambda: greet(device_id={"site": site - 1}))
    pl.when(site < sites - 1)(lambda: greet(device_id={"site": site + 1}))
    far_below, far_above = odd & (site > 1), odd & (site + 2 < sites)
    pl.when(far_below)(lambda: greet(device_id={"site": site - 2}))
    pl.when(far_above)(lambda: greet(device_id={"site": site + 2}))
    pl.when(chip > 0)(lambda: greet(device_id={"term": term - 2}))
    pl.when(chip < chips - 1)(lambda: greet(device_id={"term": term + 2}))
    bounds = (site > 0, site < sites - 1, far_below, far_above, chip > 0, chip < chips - 1)
    peers = 1
    for met in bounds:
        peers = peers + jnp.where(met, 1, 0)
    pl.semaphore_wait(barrier, peers)

    lanes = lax.broadcasted_iota(jnp.int32, coef_out.shape, 1)
    coef_out[...] = jnp.where(lanes == 0, coef[0, 0, 0], coef[0, 0, 1])

    @pl.when(leading)
    def _():
        coef_copy().start()

        @pl.loop(0, min(LEAD, nsec))
        def _(q):
            pl.when(needed(q, core))(lambda: tensor_copy(q).start())

    rows = lax.broadcasted_iota(jnp.int32, (width, width), 0)
    columns = lax.broadcasted_iota(jnp.int32, (width, width), 1)

    def framed(x, high, wide):
        return jnp.where((rows < high) & (columns < wide), x, 0.0)

    def prepare_right(h):
        held = jnp.minimum(h, nsec - 1)
        size = jnp.where(h < nsec, sizes[held], 0)
        there = pattern[0, held].astype(jnp.float32)
        rights[h % 3] = beside(framed(right_v[held], size, size) * there)

    def prepare_tensors(h):
        q = jnp.minimum(h, nsec - 1)
        before, after = jnp.maximum(q - 1, 0), jnp.minimum(q + 1, nsec - 1)
        size, size_before = sizes[q], sizes[before]
        size_after = jnp.where(q + 1 < nsec, sizes[after], 0)
        tensors[h % 2, 0] = beside(framed(mps_v[0, q], size, size).T)
        tensors[h % 2, 1] = beside(framed(mps_v[1, before], size_before, size).T)
        states[h % 2] = jnp.concatenate(
            [
                beside(framed(psi_v[0, q], size, size), 0),
                beside(framed(psi_v[1, q], size, size_after), 0),
            ],
            axis=1,
        )

    environs[1] = jnp.zeros((width, 2 * width), jnp.bfloat16)
    middles[1] = jnp.zeros((width, 2 * width), jnp.bfloat16)
    mps_copy(0).wait()
    psi_copy(0).wait()
    right_copy(0).wait()
    right_copy(1).wait()
    prepare_tensors(0)
    prepare_right(0)
    prepare_right(1)

    def receive(q):
        @pl.when(needed(q, core))
        def _():
            tensor_copy(q).wait_recv()
            swap_copy(q, core).start()

    @pl.when(odd)
    def _():
        coef_copy().wait_recv()
        receive(0)

    def advanced(blocks, q, same, step, weights):
        here = dot(as_left(blocks[q % 2]), as_right(same, 1), 1) * weights[0]
        shifted = dot(as_left(blocks[(q + 1) % 2]), as_right(step, 1), 1) * weights[1]
        return dot(
            jnp.concatenate([as_left(same), as_left(step)], axis=1),
            jnp.concatenate([as_right(beside(here, 0), 0), as_right(beside(shifted, 0), 0)], axis=0),
            0,
        )

    def update(q):
        before = jnp.maximum(q - 1, 0)
        pl.when(site < 2)(lambda: left_copy(q).wait())
        pl.when(site > 1)(lambda: e_copy(q).wait_recv())
        size, size_before = sizes[q], sizes[before]
        first = jnp.where(site < 2, pattern[0, q].astype(jnp.float32), 1.0)
        below = jnp.where(q > 0, 1.0, 0.0)
        weights = coef[0, 0, 0], coef[0, 0, 1] * below

        @pl.when(odd)
        def _():
            pl.when(needed(q, 1 - core))(lambda: swap_copy(q, 1 - core).wait_recv())
            earlier[0] = beside(framed(mps_in[0, q], size, size).T)
            earlier[1] = beside(framed(mps_in[1, before], size_before, size).T)
            environs[q % 2] = beside(framed(e_in[q], size, size) * first)
            weights_in = coef_in[0:1, 0:1], coef_in[0:1, 1:2] * below
            middle = advanced(environs, q, earlier[0], earlier[1], weights_in)
            middles[q % 2] = beside(middle)
            e_out[q] = advanced(middles, q, tensors[q % 2, 0], tensors[q % 2, 1], weights)
            pl.when(site + 1 < sites)(lambda: e_copy(q).start())
            pl.when(site + 2 < sites)(lambda: e_copy(q, 2).start())

        @pl.when(even)
        def _():
            environs[q % 2] = beside(framed(e_in[q], size, size) * first)
            e_out[q] = advanced(environs, q, tensors[q % 2, 0], tensors[q % 2, 1], weights)

    def apply(q):
        @pl.when(q + 1 < nsec)
        def _():
            mps_copy(q + 1).wait()
            psi_copy(q + 1).wait()

        pl.when(q + 2 < nsec)(lambda: right_copy(q + 2).wait())
        both = dot(as_left(beside(e_out[q])), as_right(states[q % 2], 0), 0)
        for state in (0, 1):
            value = both[:, state * width:(state + 1) * width] * coef[0, 0, 2 + state]
            value = dot(as_left(beside(value)), as_right(rights[(q + state) % 3], 1), 1)
            for i in range(in_sector):
                partial[q * in_sector + i, state] = value[i * unit:(i + 1) * unit]
        prepare_tensors(q + 1)
        prepare_right(q + 2)

        for i in range(in_sector):
            pair_copy(q * in_sector + i).start()

    def forward(q, chosen, first, arrived, copy):
        for i in range(in_sector):
            piece = q * in_sector + i
            owner_chip = piece // per // 2

            @pl.when(chosen(owner_chip))
            def _():
                pair_copy(piece).wait_recv()

                @pl.when(first)
                def _():
                    partial[piece, core] = partial[piece, core] + pair_in[piece]

                @pl.when(jnp.logical_not(first))
                def _():
                    copy(piece).wait_recv()
                    partial[piece, core] = (partial[piece, core] + pair_in[piece]) + arrived[piece]

                copy(piece).start()

    def upward(q):
        forward(q, lambda owner_chip: owner_chip > chip, chip == 0, up_in, up_copy)

    def downward(q):
        forward(q, lambda owner_chip: owner_chip < chip, chip == chips - 1, down_in, down_copy)

    def ending(q):
        for i in range(in_sector):
            piece = q * in_sector + i
            owner = piece // per

            @pl.when(owner // 2 == chip)
            def _():
                pair_copy(piece).wait_recv()
                partial[piece, core] = partial[piece, core] + pair_in[piece]

                @pl.when(chip > 0)
                def _():
                    up_copy(piece).wait_recv()
                    partial[piece, core] = partial[piece, core] + up_in[piece]

                @pl.when(chip < chips - 1)
                def _():
                    down_copy(piece).wait_recv()
                    partial[piece, core] = partial[piece, core] + down_in[piece]

                @pl.when(owner % 2 == core)
                def _():
                    target = pl.ds(pl.multiple_of((piece % per) * unit, unit), unit)
                    out[0, core, target, :] = partial[piece, core]

                pl.when(owner % 2 != core)(lambda: last_copy(piece).start())

    from_below, from_above = chip, chips - 1 - chip

    last = site + 2 >= sites

    def reduction(t):
        for stage, hops in (
            (upward, from_below),
            (downward, from_above),
            (ending, jnp.maximum(from_below, from_above)),
        ):
            q = t - FIRST_LAG - hops * HOP_LAG
            pl.when((q >= 0) & (q < nsec))(lambda: stage(q))

    def turn(t, carry):
        pl.when(last)(lambda: reduction(t))

        @pl.when(t < nsec)
        def _():
            ahead = leading & (t + LEAD < nsec) & needed(t + LEAD, core)
            pl.when(ahead)(lambda: tensor_copy(t + LEAD).start())
            update(t)
            apply(t)
            pl.when(odd & (t + 1 < nsec))(lambda: receive(t + 1))

        pl.when(jnp.logical_not(last))(lambda: reduction(t))
        return carry

    lax.fori_loop(0, nsec + FIRST_LAG + (chips - 1) * HOP_LAG, turn, 0)

    @pl.loop(0, nsec)
    def _(q):
        pl.when(odd & needed(q, core))(lambda: swap_copy(q, core).wait_send())
        pl.when(odd & (site + 1 < sites))(lambda: e_copy(q).wait_send())
        pl.when(odd & (site + 2 < sites))(lambda: e_copy(q, 2).wait_send())
        pl.when(leading & needed(q, core))(lambda: tensor_copy(q).wait_send())
        for i in range(in_sector):
            piece = q * in_sector + i
            owner_chip = piece // per // 2
            pair_copy(piece).wait_send()
            pl.when(owner_chip > chip)(lambda: up_copy(piece).wait_send())
            pl.when(owner_chip < chip)(lambda: down_copy(piece).wait_send())

    pl.when(leading)(lambda: coef_copy().wait_send())

    @pl.loop(0, per)
    def _(i):
        last_copy(i).wait()
        target = pl.ds(pl.multiple_of(i * unit, unit), unit)
        out[0, 1 - core, target, :] = last_in[i]


def shards(left_env, right_env, mps, psi, coef, sector_sizes, pattern):
    nsec, width = left_env.shape[1], left_env.shape[-1]
    sites, terms = lax.axis_size("site"), lax.axis_size("term")
    rows_owned = nsec * width // terms
    unit = math.gcd(rows_owned, width)
    pieces = nsec * width // unit
    per = rows_owned // unit
    block = (nsec, width, width)
    dma = pltpu.SemaphoreType.DMA
    hbm, smem = pl.BlockSpec(memory_space=pl.ANY), pl.BlockSpec(memory_space=pltpu.SMEM)
    return pl.pallas_call(
        functools.partial(kernel, sites, terms, unit),
        out_shape=jax.ShapeDtypeStruct((1, 2, rows_owned, width), jnp.float32),
        in_specs=[hbm] * 4 + [smem] * 3,
        out_specs=pl.BlockSpec(memory_space=pltpu.VMEM),
        scratch_shapes=[
            pltpu.VMEM(block, jnp.float32),
            pltpu.VMEM(block, jnp.float32),
            pltpu.VMEM(block, jnp.float32),
            pltpu.VMEM((2,) + block, jnp.float32),
            pltpu.VMEM((2,) + block, jnp.float32),
            pltpu.VMEM((pieces, 2, unit, width), jnp.float32),
            pltpu.VMEM((pieces, unit, width), jnp.float32),
            pltpu.VMEM((pieces, unit, width), jnp.float32),
            pltpu.VMEM((pieces, unit, width), jnp.float32),
            pltpu.VMEM((per, unit, width), jnp.float32),
            pltpu.VMEM((2, width, 2 * width), jnp.bfloat16),
            pltpu.VMEM((2, 2, width, 2 * width), jnp.bfloat16),
            pltpu.VMEM((2, 2 * width, 2 * width), jnp.bfloat16),
            pltpu.VMEM((3, width, 2 * width), jnp.bfloat16),
            pltpu.VMEM((2,) + block, jnp.float32),
            pltpu.VMEM((2, width, 2 * width), jnp.bfloat16),
            pltpu.VMEM((2, width, 2 * width), jnp.bfloat16),
            pltpu.VMEM((8, 128), jnp.float32),
            pltpu.VMEM((8, 128), jnp.float32),
            dma((nsec,)), dma((nsec,)), dma((nsec,)), dma((nsec,)),
            dma((nsec,)), dma((nsec,)),
            dma((pieces,)), dma((pieces,)), dma((pieces,)), dma((pieces,)), dma((pieces,)),
            dma((per,)), dma((per,)),
            dma((nsec,)), dma((nsec,)), dma((nsec,)), dma((nsec,)), dma((nsec,)), dma((2,)),
        ],
        compiler_params=pltpu.CompilerParams(
            collective_id=0, has_side_effects=True, vmem_limit_bytes=58 * 2**20
        ),
    )(left_env, right_env, mps, psi, coef, sector_sizes, pattern)


def solution(mesh):
    return jax.shard_map(
        shards,
        mesh=mesh,
        in_specs=(
            P("term", None, None, None),
            P("site", "term", None, None, None),
            P("site", None, None, None, None),
            P("site", None, None, None, None),
            P("site", "term", None),
            P(),
            P("term", None),
        ),
        out_specs=P("site", None, "term", None),
        check_vma=False,
    )
```
